256 devices in a mesh: img: 16 (over z_lo, y), tile: 16 (over x, z_hi, core).
Axes of the slice: x: 4, y: 4, z: 8 (z_hi: 2, z_lo: 4; z = z_hi * 4 + z_lo), core: 2. Of those that a mesh axis runs over, the one named last changes fastest.
Arguments:
- feature_map: bfloat16 [16, 256, 256, 256], P('img', 'tile'), may hold values from -0.0234375 to 0.0234375
- cotangent: bfloat16 [16, 256, 256, 256], P('img', 'tile'), may hold values from -6 to 6
- style: float32 [16, 256], P('img'), may hold values from 0.3 to 3
- bank: bfloat16 [8, 256, 9, 256], P(None, 'tile'), may hold values from -0.125 to 0.125
- selection: int32 [16, 3], P('img'), may hold values from 0 to 7, all different within a row
Outputs:
- input_grad: bfloat16 [16, 256, 256, 256], P('img', 'tile')
- style_grad: float32 [16, 256], P('img')
- bank_grad: float32 [8, 256, 9, 256], P(None, 'tile')
The draws below stay inside these ranges and needn't reach their ends.
Inputs may be any that keep to these rules, and one draw needn't show every extreme that they name: `selection`: each row names 3 different banks, and every bank is named by some image.
All inputs are finite; a program needn't handle non-finite values.
Results may differ from the reference program's by a relative error of at most 0.012.
Values may be sent and summed in bfloat16 or wider, within the bound.
No kernel may reach another device: no remote copies, remote signals or barrier semaphores. Data moves between devices by JAX's collectives and lax.ppermute only.
A program may use at most 128 MiB of HBM per device.

```python
import math
import jax
import jax.numpy as jnp
from jax import lax

C = 256
BANKS = 8
TOP = 3
MAP_W = 256
IMAGES = 16
MAP_H = 256


def block_levels(stream_key, extent, shards, low, high):
    level, own = 1.0, jax.random.fold_in(stream_key, 6)
    for dim, shards_of in shards:
        draws = jnp.exp(jax.random.uniform(jax.random.fold_in(own, dim), (shards_of,), jnp.float32, low / len(shards), high / len(shards)))
        level = level * jnp.repeat(draws, extent[dim] // shards_of).reshape([-1 if axis == dim else 1 for axis in range(len(extent))])
    return level


def distinct(key, rows, number_of, top, lift):
    order = jax.random.permutation(jax.random.fold_in(key, 1), number_of)
    pull = order
    for power in range(3):
        pull = pull * pull // number_of
    pull = pull * lift // number_of
    chance = jax.random.randint(jax.random.fold_in(key, 2), (rows, number_of), 0, 4096) + pull
    holders = jax.random.permutation(jax.random.fold_in(key, 3), rows)[jnp.arange(number_of) % rows]
    chance = jnp.where(jnp.arange(rows)[:, None] == holders[None, :], 1 << 14, chance)
    merit = chance * number_of + jnp.arange(number_of)
    return lax.top_k(merit.astype(jnp.int32), top)[1].astype(jnp.int32)


def scatter_about(key, extent, deviation, most, cuts=(), held_as=jnp.bfloat16):
    gain = block_levels(key, extent, cuts, -0.22, 0.18) if cuts else 1.0
    entries = jax.random.normal(key, extent, jnp.float32) * deviation * gain
    return jnp.minimum(jnp.maximum(entries, -most), most).astype(held_as)


def setup_inputs(seed: int = 0) -> dict:
    key_of = jax.random.split(jax.random.key(seed), 6)
    return {
        "feature_map": scatter_about(key_of[0], (IMAGES, MAP_H, MAP_W, C), (1.0 / MAP_W), 0.0234375, ((0, 16), (1, 16))),
        "cotangent": scatter_about(key_of[1], (IMAGES, MAP_H, MAP_W, C), 1.0, 6.0, ((0, 16), (1, 16))),
        "style": jnp.clip(jnp.exp(math.log(3.0) - 2.3025851 * jax.random.uniform(key_of[2], (IMAGES, C), jnp.float32) ** block_levels(key_of[2], (IMAGES, C), ((0, 16),), -0.2, 0.2)), 0.3, 3.0),
        "bank": scatter_about(key_of[3], (BANKS, C, 9, C), (9 * C) ** -0.5, 0.125, ((1, 16),)),
        "selection": distinct(key_of[4], IMAGES, BANKS, TOP, 3072),
    }


epsilon = 1e-06

def bank_mixing(selection, bank_count):
    pick_count = selection.shape[1]
    ranks = jnp.arange(pick_count).astype(jnp.float32)
    weights = (pick_count - ranks) / (pick_count * (pick_count + 1) / 2.0)
    onehot = (selection[:, :, None] == jnp.arange(bank_count, dtype=jnp.int32)[None, None, :]).astype(jnp.float32)
    return lax.optimization_barrier(jnp.sum(weights[None, :, None] * onehot, axis=1))

def one_image(args, bank):
    image, cotan, style_row, mix_row = args
    height, width, channels = image.shape
    kernel = jnp.einsum('k,kotc->otc', mix_row, bank.astype(jnp.float32))
    modded = kernel * style_row[None, None, :]
    demod_scale = lax.rsqrt(lax.optimization_barrier(jnp.sum(modded * modded, axis=(1, 2))) + epsilon)
    final_kernel = (modded * demod_scale[:, None, None]).astype(jnp.bfloat16)
    padded = jnp.pad(cotan, ((1, 1), (1, 1), (0, 0)))
    flat_in = image.reshape(height * width, channels)
    data_grad = jnp.zeros((height * width, channels), jnp.float32)
    grads = []
    for shift_row in (-1, 0, 1):
        for shift_col in (-1, 0, 1):
            tap = (shift_row + 1) * 3 + (shift_col + 1)
            moved = padded[1 - shift_row:1 - shift_row + height, 1 - shift_col:1 - shift_col + width, :]
            moved = moved.reshape(height * width, channels)
            data_grad = data_grad + jnp.dot(moved, final_kernel[:, tap, :], preferred_element_type=jnp.float32)
            grads.append(jnp.dot(moved.T, flat_in, preferred_element_type=jnp.float32))
    grad = jnp.stack(grads, axis=1)
    curvature = lax.optimization_barrier(jnp.sum(grad * modded, axis=(1, 2)))
    modded_grad = demod_scale[:, None, None] * grad - (demod_scale ** 3)[:, None, None] * modded * curvature[:, None, None]
    style_grad = lax.optimization_barrier(jnp.sum(modded_grad * kernel, axis=(0, 1)))
    kernel_grad = modded_grad * style_row[None, None, :]
    return (data_grad.astype(jnp.bfloat16).reshape(height, width, channels), style_grad, kernel_grad)

def reference(feature_map, cotangent, style, bank, selection):
    mixing = bank_mixing(selection, bank.shape[0])
    input_grad, style_grad, kernel_grads = lax.map(lambda args: one_image(args, bank), (feature_map, cotangent, style, mixing))
    bank_grad = jnp.einsum('bk,botc->kotc', mixing, kernel_grads)
    return (input_grad, style_grad, bank_grad)
```

```python
import functools

import jax
import jax.numpy as jnp
from jax import lax
from jax.experimental import pallas as pl
from jax.experimental.pallas import tpu as pltpu
from jax.sharding import PartitionSpec as P

epsilon = 1e-06
F32 = jnp.float32
BF16 = jnp.bfloat16
VMEM = pl.BlockSpec(memory_space=pltpu.VMEM)
SMEM = pl.BlockSpec(memory_space=pltpu.SMEM)
ANY = pl.BlockSpec(memory_space=pl.ANY)

NX, NZ, NC = 4, 2, 2
NL, NY = 4, 4


def tile_perm(move):
    place = lambda x, z, c: (x * NZ + z) * NC + c
    return [
        (place(x, z, c), place(*move(x, z, c)))
        for x in range(NX)
        for z in range(NZ)
        for c in range(NC)
    ]


def img_perm(move):
    place = lambda l, y: l * NY + y
    return [(place(l, y), place(*move(l, y))) for l in range(NL) for y in range(NY)]


def swap_core(a):
    return lax.ppermute(a, "tile", tile_perm(lambda x, z, c: (x, z, 1 - c)))


def swap_z(a):
    return lax.ppermute(a, "tile", tile_perm(lambda x, z, c: (x, 1 - z, c)))


def shift_x(a, k):
    return lax.ppermute(a, "tile", tile_perm(lambda x, z, c: ((x + k) % NX, z, c)))


def flip_x(a, k):
    return lax.ppermute(a, "tile", tile_perm(lambda x, z, c: (x ^ k, z, c)))


def flip_l(a, k):
    return lax.ppermute(a, "img", img_perm(lambda l, y: (l ^ k, y)))


def shift_y(a, k):
    return lax.ppermute(a, "img", img_perm(lambda l, y: (l, (y + k) % NY)))


def call(body, outs, in_specs, scratch=(), flops=0, nbytes=0, vmem=48 << 20, name=None):
    return pl.pallas_call(
        body,
        out_shape=outs,
        in_specs=in_specs,
        out_specs=jax.tree.map(lambda _: VMEM, outs),
        scratch_shapes=list(scratch),
        compiler_params=pltpu.CompilerParams(vmem_limit_bytes=vmem),
        cost_estimate=pl.CostEstimate(flops=flops, bytes_accessed=nbytes, transcendentals=0),
        name=name,
    )


def shape(s, dtype):
    return jax.ShapeDtypeStruct(s, dtype)


def demod_of(kernel, style):
    total = None
    for t in range(kernel.shape[0]):
        modded = kernel[t] * style
        total = modded * modded if total is None else total + modded * modded
    return lax.rsqrt(jnp.sum(total, axis=1, keepdims=True) + epsilon)


def mix_body(sel, style, bank, kernel, final):
    banks, taps = bank.shape[:2]
    top = sel.shape[1]
    weights = []
    for k in range(banks):
        w = F32(0)
        for j in range(top):
            w = w + jnp.where(sel[0, j] == k, F32((top - j) / (top * (top + 1) / 2)), F32(0))
        weights.append(w)
    for t in range(taps):
        mixed = None
        for k in range(banks):
            term = weights[k] * bank[k, t].astype(F32)
            mixed = term if mixed is None else mixed + term
        kernel[t] = mixed
    demod = demod_of(kernel, style[...])
    for t in range(taps):
        final[t] = (kernel[t] * style[...] * demod).astype(BF16)


def moved_columns(row):
    width = row.shape[0]
    column = lax.broadcasted_iota(jnp.int32, row.shape, 0)
    before = jnp.where(column == 0, F32(0), pltpu.roll(row, 1, 0))
    after = jnp.where(column == width - 1, F32(0), pltpu.roll(row, width - 1, 0))
    return before, after


def turned(row, core, out, at):
    width, channels = row.shape
    groups = channels // (16 * NC)
    flat = jnp.transpose(row)
    for g in range(groups):
        for c in range(NC):
            start = (g * NC + c) * 16
            out[c ^ core, g, :, at] = flat[start : start + 16]


def grad_body(place, cot, fm, grad, cot_t, fm_v):
    rows, width, channels = cot.shape
    groups = channels // (16 * NC)
    core = place[2]
    pad = jnp.zeros((width, channels), BF16)
    for v in range(3):
        fm_v[v, pl.ds(0, width)] = pad
        fm_v[v, pl.ds((rows + 1) * width, width)] = pad

    @pl.loop(0, rows)
    def _(r):
        row = fm[r]
        before, after = moved_columns(row.astype(F32))
        here = pl.ds(pl.multiple_of((r + 1) * width, width), width)
        fm_v[0, here] = before.astype(BF16)
        fm_v[1, here] = row
        fm_v[2, here] = after.astype(BF16)
        turned(cot[r], core, cot_t, pl.ds(pl.multiple_of(r * width, width), width))

    @pl.loop(0, 9)
    def _(t):
        u, v = t // 3, t % 3
        left = cot_t[...].reshape(channels, rows * width)
        right = fm_v[v, pl.ds(pl.multiple_of(u * width, width), rows * width)]
        out = jnp.dot(left, right, preferred_element_type=F32)
        grad[t] = out.reshape(NC, groups, 16, channels)


def edge_body(place, grad, low, high, first, last, mine, theirs, turn_low, turn_high):
    taps, _, groups, _, channels = grad.shape
    width = low.shape[0]
    core = place[2]
    turned(low[...], core, turn_low, pl.ds(0, width))
    turned(high[...], core, turn_high, pl.ds(0, width))

    def put(t, value):
        for g in range(groups):
            mine[g, t] = value[0, g]
            theirs[g, t] = value[1, g].astype(BF16)

    for turn, row, tap in ((turn_high, last, 0), (turn_low, first, 6)):
        whole = row[...].reshape(width, channels)
        before, after = moved_columns(whole.astype(F32))
        left = turn[...].reshape(channels, width)
        for v, right in enumerate((before.astype(BF16), whole, after.astype(BF16))):
            out = jnp.dot(left, right, preferred_element_type=F32)
            put(tap + v, grad[tap + v] + out.reshape(NC, groups, 16, channels))
    for t in (3, 4, 5):
        put(t, grad[t])


def split_x_body(place, mine, got, own, one, two, three):
    x = place[0]
    for k, out in ((0, own), (1, one), (2, two), (3, three)):
        base = lax.rem(x + k, NX) * NZ
        for z in range(NZ):
            out[z] = (mine[base + z] + got[base + z].astype(F32)).astype(out.dtype)


def split_z_body(place, mine, one, two, three, own, other):
    z = place[1]
    for k, out in ((0, own), (1, other)):
        at = z ^ k
        total = mine[at] + one[at].astype(F32) + two[at].astype(F32) + three[at].astype(F32)
        out[...] = total.astype(out.dtype)


def owner_body(sel, style, kernel, mine, got, message, style_part):
    taps, outs, channels = kernel.shape
    top = sel.shape[1]
    s = style[...]
    demod = demod_of(kernel, s)
    total = None
    for t in range(taps):
        grad = mine[t] + got[t].astype(F32)
        term = grad * (kernel[t] * s)
        total = term if total is None else total + term
    curvature = jnp.sum(total, axis=1, keepdims=True)
    slope = demod * demod * demod * curvature
    part = None
    for t in range(taps):
        grad = mine[t] + got[t].astype(F32)
        modded_grad = demod * grad - slope * (kernel[t] * s)
        term = modded_grad * kernel[t]
        part = term if part is None else part + term
        message[t] = (modded_grad * s).astype(BF16)
    style_part[...] = jnp.broadcast_to(jnp.sum(part, axis=0, keepdims=True), style_part.shape)
    bank = lax.broadcasted_iota(jnp.int32, (outs, channels), 0)
    rank = jnp.zeros((outs, channels), F32)
    for j in range(top):
        rank = rank + jnp.where(bank == sel[0, j], F32(top - j), F32(0))
    message[taps] = rank.astype(BF16)


def banks_body(*refs):
    out = refs[-1]
    banks, taps = out.shape[:2]
    pieces = []
    for ref in refs[:-1]:
        if len(ref.shape) == 3:
            pieces.append(ref)
        else:
            pieces.extend(ref.at[n] for n in range(ref.shape[0]))
    weights = [piece[taps].astype(F32) / F32(6) for piece in pieces]

    @pl.loop(0, taps)
    def _(t):
        values = [piece[t].astype(F32) for piece in pieces]
        for k in range(banks):
            total = None
            for weight, value in zip(weights, values):
                term = weight[k : k + 1] * value
                total = term if total is None else total + term
            out[k, t] = total


def input_body(place, near, far, low, high, cot, out, final, padded, sem):
    rows, width, channels = out.shape
    copy = pltpu.make_async_copy(cot, padded.at[pl.ds(1, rows)], sem)
    copy.start()
    padded[0] = low[...]
    padded[rows + 1] = high[...]
    x, z, core = place[0], place[1], place[2]
    for n in range(NX * NZ):
        at = lax.rem(x + NX - n // NZ, NX) * NZ + (z ^ (n % NZ))
        for pieces, c in ((near, core), (far, 1 - core)):
            for t in range(9):
                u, v = t // 3, t % 3
                final[u, pl.ds(pl.multiple_of((at * NC + c) * 16, 16), 16), v * channels : (v + 1) * channels] = pieces[n, t]
    copy.wait()
    step = 2

    @pl.loop(0, rows // step)
    def _(q):
        r = q * step
        left = jnp.concatenate(
            [padded[pl.ds(r + 2 - u, step)].reshape(step * width, channels) for u in range(3)], axis=1
        )
        right = final[...].reshape(3 * channels, 3 * channels)
        sums = jnp.dot(left, right, preferred_element_type=F32)
        for n in range(step):
            part = sums[n * width : (n + 1) * width]
            _, after = moved_columns(part[:, :channels])
            before, _ = moved_columns(part[:, 2 * channels :])
            out[r + n] = (part[:, channels : 2 * channels] + after + before).astype(BF16)


def local(feature_map, cotangent, style, bank, selection):
    _, rows, width, channels = feature_map.shape
    fm = feature_map.reshape(rows, width, channels)
    cot = cotangent.reshape(rows, width, channels)
    banks, own_out, taps, _ = bank.shape
    groups = NX * NZ
    tile = lax.axis_index("tile")
    place = jnp.stack([tile // (NZ * NC), (tile // NC) % NZ, tile % NC]).astype(jnp.int32)

    count = lax.axis_size("tile")
    low = lax.ppermute(cot[rows - 1], "tile", [(i, i + 1) for i in range(count - 1)])
    high = lax.ppermute(cot[0], "tile", [(i + 1, i) for i in range(count - 1)])

    piece = (taps, own_out, channels)
    kernel, final = call(
        mix_body, (shape(piece, F32), shape(piece, BF16)), [SMEM, VMEM, VMEM], flops=10**6, nbytes=10**6, name="mix"
    )(selection, style, jnp.transpose(bank, (0, 2, 1, 3)))

    final_z = swap_z(final)
    near = [final, final_z]
    for k in range(1, NX):
        near += [shift_x(final, k), shift_x(final_z, k)]
    near = jnp.stack(near)
    far = swap_core(near)

    grad = call(
        grad_body,
        shape((taps, NC, groups, 16, channels), F32),
        [SMEM, VMEM, VMEM],
        [
            pltpu.VMEM((NC, groups, 16, rows * width), BF16),
            pltpu.VMEM((3, (rows + 2) * width, channels), BF16),
        ],
        flops=2 * 9 * rows * width * channels * channels,
        nbytes=4 * rows * width * channels,
        name="grad",
    )(place, cot, fm)
    mine, theirs = call(
        edge_body,
        (shape((groups,) + piece, F32), shape((groups,) + piece, BF16)),
        [SMEM] + [VMEM] * 5,
        [pltpu.VMEM((NC, groups, 16, width), BF16)] * 2,
        flops=2 * 6 * width * channels * channels,
        nbytes=4 * 10**6,
        name="edge",
    )(place, grad, low, high, fm[0], fm[rows - 1])

    pair = (NZ,) + piece
    own_x, one, two, three = call(
        split_x_body,
        (shape(pair, F32),) + (shape(pair, BF16),) * 3,
        [SMEM, VMEM, VMEM],
        flops=10**6,
        nbytes=3 * 10**6,
        name="split_x",
    )(place, mine, swap_core(theirs))
    own_z, other = call(
        split_z_body,
        (shape(piece, F32), shape(piece, BF16)),
        [SMEM] + [VMEM] * 4,
        flops=10**6,
        nbytes=10**6,
        name="split_z",
    )(place, own_x, shift_x(one, 1), shift_x(two, 2), shift_x(three, 3))
    message, style_part = call(
        owner_body,
        (shape((taps + 1, own_out, channels), BF16), shape((8, channels), F32)),
        [SMEM] + [VMEM] * 4,
        flops=10**6,
        nbytes=10**6,
        name="owner",
    )(selection, style, kernel, own_z, swap_z(other))

    over_l = [flip_l(message, k) for k in range(1, NL)]
    over_y = [shift_y(message, k) for k in range(1, NY)]
    ahead = jnp.stack(over_l)
    rest = [shift_y(ahead, k) for k in range(1, NY)]

    style_sum = style_part + swap_core(style_part)
    style_sum = style_sum + flip_x(style_sum, 1)
    style_sum = style_sum + flip_x(style_sum, 2)
    style_sum = style_sum + swap_z(style_sum)

    bank_grad = call(
        banks_body,
        shape((banks,) + piece, F32),
        [VMEM] * 10,
        flops=10**7,
        nbytes=3 * 10**6,
        name="banks",
    )(message, *over_l, *over_y, *rest)

    input_grad = call(
        input_body,
        shape((rows, width, channels), BF16),
        [SMEM] + [VMEM] * 4 + [ANY],
        [
            pltpu.VMEM((3, channels, 3 * channels), BF16),
            pltpu.VMEM((rows + 2, width, channels), BF16),
            pltpu.SemaphoreType.DMA,
        ],
        flops=2 * 9 * rows * width * channels * channels,
        nbytes=4 * rows * width * channels,
        name="input",
    )(place, near, far, low, high, cot)

    return (
        input_grad.reshape(feature_map.shape),
        style_sum[:1],
        jnp.transpose(bank_grad, (0, 2, 1, 3)),
    )


def solution(mesh):
    in_specs = (
        P("img", "tile", None, None),
        P("img", "tile", None, None),
        P("img", None),
        P(None, "tile", None, None),
        P("img", None),
    )
    out_specs = (P("img", "tile", None, None), P("img", None), P(None, "tile", None, None))
    return jax.shard_map(local, mesh=mesh, in_specs=in_specs, out_specs=out_specs, check_vma=False)
```

```python
import functools

import jax
import jax.numpy as jnp
from jax import lax
from jax.experimental import pallas as pl
from jax.experimental.pallas import tpu as pltpu
from jax.sharding import PartitionSpec as P

epsilon = 1e-06
F32 = jnp.float32
BF16 = jnp.bfloat16
VMEM = pl.BlockSpec(memory_space=pltpu.VMEM)
SMEM = pl.BlockSpec(memory_space=pltpu.SMEM)
ANY = pl.BlockSpec(memory_space=pl.ANY)
HBM = pl.BlockSpec(memory_space=pltpu.HBM)

NX, NZ, NC = 4, 2, 2
NL, NY = 4, 4


def tile_perm(move):
    place = lambda x, z, c: (x * NZ + z) * NC + c
    return [
        (place(x, z, c), place(*move(x, z, c)))
        for x in range(NX)
        for z in range(NZ)
        for c in range(NC)
    ]


def img_perm(move):
    place = lambda l, y: l * NY + y
    return [(place(l, y), place(*move(l, y))) for l in range(NL) for y in range(NY)]


def swap_core(a):
    return lax.ppermute(a, "tile", tile_perm(lambda x, z, c: (x, z, 1 - c)))


def swap_z(a):
    return lax.ppermute(a, "tile", tile_perm(lambda x, z, c: (x, 1 - z, c)))


def shift_x(a, k):
    return lax.ppermute(a, "tile", tile_perm(lambda x, z, c: ((x + k) % NX, z, c)))


def flip_x(a, k):
    return lax.ppermute(a, "tile", tile_perm(lambda x, z, c: (x ^ k, z, c)))


def flip_l(a, k):
    return lax.ppermute(a, "img", img_perm(lambda l, y: (l ^ k, y)))


def shift_y(a, k):
    return lax.ppermute(a, "img", img_perm(lambda l, y: (l, (y + k) % NY)))


def call(body, outs, in_specs, scratch=(), flops=0, nbytes=0, vmem=16 << 20, name=None):
    return pl.pallas_call(
        body,
        out_shape=outs,
        in_specs=in_specs,
        out_specs=jax.tree.map(lambda _: VMEM, outs),
        scratch_shapes=list(scratch),
        compiler_params=pltpu.CompilerParams(vmem_limit_bytes=vmem),
        cost_estimate=pl.CostEstimate(flops=flops, bytes_accessed=nbytes, transcendentals=0),
        name=name,
    )


def shape(s, dtype):
    return jax.ShapeDtypeStruct(s, dtype)


def demod_of(kernel, style):
    total = None
    for t in range(kernel.shape[0]):
        modded = kernel[t] * style
        total = modded * modded if total is None else total + modded * modded
    return lax.rsqrt(jnp.sum(total, axis=1, keepdims=True) + epsilon)


def fetch(copies):
    for copy in copies:
        copy.start()
    for copy in copies:
        copy.wait()


def rows_body(cot, last, first, sems):
    fetch(
        [
            pltpu.make_async_copy(cot.at[cot.shape[0] - 1], last, sems.at[0]),
            pltpu.make_async_copy(cot.at[0], first, sems.at[1]),
        ]
    )


def mix_body(sel, style, bank, after, kernel, final):
    del after
    banks, taps = bank.shape[:2]
    top = sel.shape[1]
    weights = []
    for k in range(banks):
        w = F32(0)
        for j in range(top):
            w = w + jnp.where(sel[0, j] == k, F32((top - j) / (top * (top + 1) / 2)), F32(0))
        weights.append(w)
    for t in range(taps):
        mixed = None
        for k in range(banks):
            term = weights[k] * bank[k, t].astype(F32)
            mixed = term if mixed is None else mixed + term
        kernel[t] = mixed
    demod = demod_of(kernel, style[...])
    for t in range(taps):
        final[t] = (kernel[t] * style[...] * demod).astype(BF16)


def moved_columns(row):
    width = row.shape[0]
    column = lax.broadcasted_iota(jnp.int32, row.shape, 0)
    before = jnp.where(column == 0, F32(0), pltpu.roll(row, 1, 0))
    after = jnp.where(column == width - 1, F32(0), pltpu.roll(row, width - 1, 0))
    return before, after


def turned(row, core, out, at):
    width, channels = row.shape
    groups = channels // (16 * NC)
    flat = jnp.transpose(row)
    for g in range(groups):
        for c in range(NC):
            start = (g * NC + c) * 16
            out[c ^ core, g, :, at] = flat[start : start + 16]


def grad_body(place, cot_hbm, fm_hbm, grad, cot, fm, cot_t, fm_v, sems, step=4):
    rows, width, channels = cot.shape
    groups = channels // (16 * NC)
    core = place[2]
    parts = rows // step
    copies = []
    for q in range(parts):
        here = pl.ds(q * step, step)
        copies.append(
            (
                pltpu.make_async_copy(cot_hbm.at[here], cot.at[here], sems.at[0, q]),
                pltpu.make_async_copy(fm_hbm.at[here], fm.at[here], sems.at[1, q]),
            )
        )
    for pair in copies:
        for copy in pair:
            copy.start()
    nothing = jnp.zeros((NC, groups, 16, width), BF16)
    cot_t[:, :, :, :width] = nothing
    cot_t[:, :, :, (rows + 1) * width :] = nothing

    def prepare(q):
        for copy in copies[q]:
            copy.wait()
        for r in range(q * step, (q + 1) * step):
            row = fm[r]
            before, after = moved_columns(row.astype(F32))
            here = pl.ds(r * width, width)
            fm_v[0, here] = before.astype(BF16)
            fm_v[1, here] = row
            fm_v[2, here] = after.astype(BF16)
            turned(cot[r], core, cot_t, pl.ds((r + 1) * width, width))

    def add(q):
        for u in range(3):
            left = cot_t[:, :, :, pl.ds((q * step + 2 - u) * width, step * width)]
            left = left.reshape(channels, step * width)
            for v in range(3):
                right = fm_v[v, pl.ds(q * step * width, step * width)]
                out = jnp.dot(left, right, preferred_element_type=F32)
                out = out.reshape(NC, groups, 16, channels)
                grad[3 * u + v] = out if q == 0 else grad[3 * u + v] + out

    prepare(0)
    for q in range(parts):
        if q + 1 < parts:
            prepare(q + 1)
        add(q)


def edge_body(place, grad, low, high, fm, after, mine, theirs, turn_low, turn_high, first, last, sems):
    del after
    taps, _, groups, _, channels = grad.shape
    copies = [
        pltpu.make_async_copy(fm.at[0], first, sems.at[0]),
        pltpu.make_async_copy(fm.at[fm.shape[0] - 1], last, sems.at[1]),
    ]
    for copy in copies:
        copy.start()
    width = low.shape[0]
    core = place[2]
    turned(low[...], core, turn_low, pl.ds(0, width))
    turned(high[...], core, turn_high, pl.ds(0, width))

    def put(t, value):
        for g in range(groups):
            mine[g, t] = value[0, g]
            theirs[g, t] = value[1, g].astype(BF16)

    for t in (3, 4, 5):
        put(t, grad[t])
    for copy in copies:
        copy.wait()
    for turn, row, tap in ((turn_high, last, 0), (turn_low, first, 6)):
        whole = row[...].reshape(width, channels)
        before, after = moved_columns(whole.astype(F32))
        left = turn[...].reshape(channels, width)
        for v, right in enumerate((before.astype(BF16), whole, after.astype(BF16))):
            out = jnp.dot(left, right, preferred_element_type=F32)
            put(tap + v, grad[tap + v] + out.reshape(NC, groups, 16, channels))


def split_x_body(place, mine, got, final, final_c, own, one, two, three, both):
    both[0] = final[...]
    both[1] = final_c[...]
    x = place[0]
    for k, out in ((0, own), (1, one), (2, two), (3, three)):
        base = lax.rem(x + k, NX) * NZ
        for z in range(NZ):
            out[z] = (mine[base + z] + got[base + z].astype(F32)).astype(out.dtype)


def split_z_body(place, mine, one, two, three, total, other):
    z = place[1]
    for k in range(NZ):
        at = z ^ k
        value = mine[at] + one[at].astype(F32) + two[at].astype(F32) + three[at].astype(F32)
        total[k] = value
        if k == 1:
            other[...] = value.astype(BF16)


def style_body(style, total, near, got, part, four):
    taps, outs, channels = total.shape[1:]
    share = jnp.zeros((outs, channels), F32)
    for k, source in enumerate((near, got)):
        dot = jnp.zeros((outs, channels), F32)
        for t in range(taps):
            dot = dot + total[k, t] * source[0, t].astype(F32)
        dot = jnp.sum(dot, axis=1, keepdims=True)
        for t in range(taps):
            final = source[0, t].astype(F32)
            share = share + (total[k, t] - final * dot) * final
    row = jnp.sum(share, axis=0, keepdims=True) / style[...]
    part[...] = jnp.broadcast_to(row, part.shape)
    four[pl.ds(0, NC)] = near[...]
    four[pl.ds(NC, NC)] = got[...]


def owner_body(sel, style, kernel, total, got, message):
    taps, outs, channels = kernel.shape
    top = sel.shape[1]
    s = style[...]
    demod = demod_of(kernel, s)
    dot = jnp.zeros((outs, channels), F32)
    for t in range(taps):
        grad = total[0, t] + got[t].astype(F32)
        dot = dot + grad * (kernel[t] * s)
    curvature = jnp.sum(dot, axis=1, keepdims=True)
    slope = demod * demod * demod * curvature
    for t in range(taps):
        grad = total[0, t] + got[t].astype(F32)
        modded_grad = demod * grad - slope * (kernel[t] * s)
        message[t] = (modded_grad * s).astype(BF16)
    bank = lax.broadcasted_iota(jnp.int32, (outs, channels), 0)
    rank = jnp.zeros((outs, channels), F32)
    for j in range(top):
        rank = rank + jnp.where(bank == sel[0, j], F32(top - j), F32(0))
    message[taps] = rank.astype(BF16)


def ahead_body(one, two, three, out):
    for k, piece in enumerate((one, two, three)):
        out[k] = piece[...]


def banks_body(*refs):
    out, both, sems = refs[-3:]
    banks, taps, outs, channels = out.shape
    pieces = []
    for ref in refs[:-3]:
        if len(ref.shape) == 3:
            pieces.append(ref)
        else:
            pieces.extend(ref.at[n] for n in range(ref.shape[0]))
    lane = lax.broadcasted_iota(jnp.int32, (outs, channels), 1)
    row = lax.broadcasted_iota(jnp.int32, (outs, channels), 0)
    ranks = jnp.zeros((outs, channels), F32)
    for n, piece in enumerate(pieces):
        ranks = jnp.where(lane // outs == n, piece[taps].astype(F32), ranks)
    left = jnp.concatenate(
        [jnp.where(lane % outs == row, ranks[k : k + 1], F32(0)) for k in range(banks)], axis=0
    ).astype(BF16)
    copies = []
    for t in range(taps):
        right = jnp.concatenate([piece[t] for piece in pieces], axis=0)
        total = jnp.dot(left, right, preferred_element_type=F32) / F32(6)
        both[:, t] = total.reshape(banks, outs, channels)
        copy = pltpu.make_async_copy(both.at[:, t], out.at[:, t], sems.at[t])
        copy.start()
        copies.append(copy)
    for copy in copies:
        copy.wait()


def input_body(place, *refs):
    finals = refs[:NX]
    low, high, cot, after, out, final, padded, sem = refs[NX:]
    del after
    rows, width, channels = out.shape
    copy = pltpu.make_async_copy(cot, padded.at[pl.ds(1, rows)], sem)
    copy.start()
    padded[0] = low[...]
    padded[rows + 1] = high[...]
    x, z, core = place[0], place[1], place[2]
    for k in range(NX):
        for n in range(NZ):
            for c in range(NC):
                at = (lax.rem(x + NX - k, NX) * NZ + (z ^ n)) * NC + (core ^ c)
                here = pl.ds(pl.multiple_of(at * 16, 16), 16)
                for t in range(9):
                    u, v = t // 3, t % 3
                    final[u, here, v * channels : (v + 1) * channels] = finals[k][n * NC + c, t]
    copy.wait()
    step = 2

    @pl.loop(0, rows // step)
    def _(q):
        r = q * step
        left = jnp.concatenate(
            [padded[pl.ds(r + 2 - u, step)].reshape(step * width, channels) for u in range(3)], axis=1
        )
        right = final[...].reshape(3 * channels, 3 * channels)
        sums = jnp.dot(left, right, preferred_element_type=F32)
        for n in range(step):
            part = sums[n * width : (n + 1) * width]
            _, after = moved_columns(part[:, :channels])
            before, _ = moved_columns(part[:, 2 * channels :])
            out[r + n] = (part[:, channels : 2 * channels] + after + before).astype(BF16)


def local(feature_map, cotangent, style, bank, selection):
    _, rows, width, channels = feature_map.shape
    fm = feature_map.reshape(rows, width, channels)
    cot = cotangent.reshape(rows, width, channels)
    banks, own_out, taps, _ = bank.shape
    groups = NX * NZ
    tile = lax.axis_index("tile")
    place = jnp.stack([tile // (NZ * NC), (tile // NC) % NZ, tile % NC]).astype(jnp.int32)
    dma = pltpu.SemaphoreType.DMA
    piece = (taps, own_out, channels)
    pair = (NZ,) + piece

    last, first = call(
        rows_body, (shape((width, channels), BF16),) * 2, [HBM], [dma((2,))], nbytes=10**6, vmem=60 << 20, name="rows"
    )(cot)
    count = lax.axis_size("tile")
    low = lax.ppermute(last, "tile", [(i, i + 1) for i in range(count - 1)])
    high = lax.ppermute(first, "tile", [(i + 1, i) for i in range(count - 1)])

    kernel, final = call(
        mix_body, (shape(piece, F32), shape(piece, BF16)), [SMEM, VMEM, VMEM, VMEM], flops=10**6, nbytes=10**6, name="mix"
    )(selection, style, jnp.transpose(bank, (0, 2, 1, 3)), last)
    final_c = swap_core(final)

    grad = call(
        grad_body,
        shape((taps, NC, groups, 16, channels), F32),
        [SMEM, HBM, HBM],
        [
            pltpu.VMEM((rows, width, channels), BF16),
            pltpu.VMEM((rows, width, channels), BF16),
            pltpu.VMEM((NC, groups, 16, (rows + 2) * width), BF16),
            pltpu.VMEM((3, rows * width, channels), BF16),
            dma((2, 4)),
        ],
        flops=2 * 9 * rows * width * channels * channels,
        nbytes=4 * rows * width * channels,
        vmem=50 << 20,
        name="grad",
    )(place, cot, fm)
    mine, theirs = call(
        edge_body,
        (shape((groups,) + piece, F32), shape((groups,) + piece, BF16)),
        [SMEM] + [VMEM] * 3 + [HBM, VMEM],
        [pltpu.VMEM((NC, groups, 16, width), BF16)] * 2 + [pltpu.VMEM((width, channels), BF16)] * 2 + [dma((2,))],
        flops=2 * 6 * width * channels * channels,
        nbytes=4 * 10**6,
        vmem=50 << 20,
        name="edge",
    )(place, grad, low, high, fm, final_c)

    own_x, one, two, three, both = call(
        split_x_body,
        (shape(pair, F32),) + (shape(pair, BF16),) * 3 + (shape((NC,) + piece, BF16),),
        [SMEM] + [VMEM] * 4,
        flops=10**6,
        nbytes=3 * 10**6,
        name="split_x",
    )(place, mine, swap_core(theirs), final, final_c)
    got_z = swap_z(both)
    total, other = call(
        split_z_body,
        (shape(pair, F32), shape(piece, BF16)),
        [SMEM] + [VMEM] * 4,
        flops=10**6,
        nbytes=10**6,
        name="split_z",
    )(place, own_x, shift_x(one, 1), shift_x(two, 2), shift_x(three, 3))
    message = call(
        owner_body,
        shape((taps + 1, own_out, channels), BF16),
        [SMEM] + [VMEM] * 4,
        flops=10**6,
        nbytes=10**6,
        name="owner",
    )(selection, style, kernel, total, swap_z(other))
    style_part, four = call(
        style_body,
        (shape((8, channels), F32), shape((NZ * NC,) + piece, BF16)),
        [VMEM] * 4,
        flops=10**9,
        nbytes=10**7,
        name="style",
    )(style, total, both, got_z)

    finals = [four] + [shift_x(four, k) for k in range(1, NX)]

    over_l = [flip_l(message, k) for k in range(1, NL)]
    over_y = [shift_y(message, k) for k in range(1, NY)]
    ahead = call(ahead_body, shape((3, taps + 1, own_out, channels), BF16), [VMEM] * 3, name="ahead")(*over_l)
    rest = [shift_y(ahead, k) for k in range(1, NY)]

    style_sum = style_part + swap_core(style_part)
    style_sum = style_sum + flip_x(style_sum, 1)
    style_sum = style_sum + flip_x(style_sum, 2)
    style_sum = style_sum + swap_z(style_sum)

    input_grad = call(
        input_body,
        shape((rows, width, channels), BF16),
        [SMEM] + [VMEM] * (NX + 2) + [HBM, VMEM],
        [
            pltpu.VMEM((3, channels, 3 * channels), BF16),
            pltpu.VMEM((rows + 2, width, channels), BF16),
            dma,
        ],
        flops=2 * 9 * rows * width * channels * channels,
        nbytes=4 * rows * width * channels,
        vmem=50 << 20,
        name="input",
    )(place, *finals, low, high, cot, ahead)

    bank_grad = pl.pallas_call(
        banks_body,
        out_shape=shape((banks,) + piece, F32),
        in_specs=[VMEM] * 10,
        out_specs=HBM,
        scratch_shapes=[pltpu.VMEM((banks,) + piece, F32), dma((taps,))],
        compiler_params=pltpu.CompilerParams(vmem_limit_bytes=16 << 20),
        cost_estimate=pl.CostEstimate(flops=10**7, bytes_accessed=3 * 10**6, transcendentals=0),
        name="banks",
    )(message, *over_l, *over_y, *rest)

    return (
        input_grad.reshape(feature_map.shape),
        style_sum[:1],
        jnp.transpose(bank_grad, (0, 2, 1, 3)),
    )


def solution(mesh):
    in_specs = (
        P("img", "tile", None, None),
        P("img", "tile", None, None),
        P("img", None),
        P(None, "tile", None, None),
        P("img", None),
    )
    out_specs = (P("img", "tile", None, None), P("img", None), P(None, "tile", None, None))
    return jax.shard_map(local, mesh=mesh, in_specs=in_specs, out_specs=out_specs, check_vma=False)
```

```python
import functools

import jax
import jax.numpy as jnp
from jax import lax
from jax.experimental import pallas as pl
from jax.experimental.pallas import tpu as pltpu
from jax.sharding import PartitionSpec as P

epsilon = 1e-06
F32 = jnp.float32
BF16 = jnp.bfloat16
VMEM = pl.BlockSpec(memory_space=pltpu.VMEM)
SMEM = pl.BlockSpec(memory_space=pltpu.SMEM)
ANY = pl.BlockSpec(memory_space=pl.ANY)
HBM = pl.BlockSpec(memory_space=pltpu.HBM)

NX, NZ, NC = 4, 2, 2
NL, NY = 4, 4


def tile_perm(move):
    place = lambda x, z, c: (x * NZ + z) * NC + c
    return [
        (place(x, z, c), place(*move(x, z, c)))
        for x in range(NX)
        for z in range(NZ)
        for c in range(NC)
    ]


def img_perm(move):
    place = lambda l, y: l * NY + y
    return [(place(l, y), place(*move(l, y))) for l in range(NL) for y in range(NY)]


def swap_core(a):
    return lax.ppermute(a, "tile", tile_perm(lambda x, z, c: (x, z, 1 - c)))


def swap_z(a):
    return lax.ppermute(a, "tile", tile_perm(lambda x, z, c: (x, 1 - z, c)))


def shift_x(a, k):
    return lax.ppermute(a, "tile", tile_perm(lambda x, z, c: ((x + k) % NX, z, c)))


def flip_x(a, k):
    return lax.ppermute(a, "tile", tile_perm(lambda x, z, c: (x ^ k, z, c)))


def flip_l(a, k):
    return lax.ppermute(a, "img", img_perm(lambda l, y: (l ^ k, y)))


def shift_y(a, k):
    return lax.ppermute(a, "img", img_perm(lambda l, y: (l, (y + k) % NY)))


def call(body, outs, in_specs, scratch=(), flops=0, nbytes=0, vmem=16 << 20, name=None):
    return pl.pallas_call(
        body,
        out_shape=outs,
        in_specs=in_specs,
        out_specs=jax.tree.map(lambda _: VMEM, outs),
        scratch_shapes=list(scratch),
        compiler_params=pltpu.CompilerParams(vmem_limit_bytes=vmem),
        cost_estimate=pl.CostEstimate(flops=flops, bytes_accessed=nbytes, transcendentals=0),
        name=name,
    )


def shape(s, dtype):
    return jax.ShapeDtypeStruct(s, dtype)


def demod_of(kernel, style):
    total = None
    for t in range(kernel.shape[0]):
        modded = kernel[t] * style
        total = modded * modded if total is None else total + modded * modded
    return lax.rsqrt(jnp.sum(total, axis=1, keepdims=True) + epsilon)


def fetch(copies):
    for copy in copies:
        copy.start()
    for copy in copies:
        copy.wait()


def rows_body(cot, last, first, sems):
    rows, width = cot.shape[:2]
    parts = sems.shape[1]
    copies = []
    for n, (row, out) in enumerate(((rows - 1, last), (0, first))):
        for p in range(parts):
            here = pl.ds(p * (width // parts), width // parts)
            copies.append(pltpu.make_async_copy(cot.at[row, here], out.at[here], sems.at[n, p]))
    fetch(copies)


def mix_body(sel, style, bank, kernel, final):
    banks, taps = bank.shape[:2]
    top = sel.shape[1]
    weights = []
    for k in range(banks):
        w = F32(0)
        for j in range(top):
            w = w + jnp.where(sel[0, j] == k, F32((top - j) / (top * (top + 1) / 2)), F32(0))
        weights.append(w)
    for t in range(taps):
        mixed = None
        for k in range(banks):
            term = weights[k] * bank[k, t].astype(F32)
            mixed = term if mixed is None else mixed + term
        kernel[t] = mixed
    demod = demod_of(kernel, style[...])
    for t in range(taps):
        final[t] = (kernel[t] * style[...] * demod).astype(BF16)


def moved_columns(row):
    width = row.shape[0]
    column = lax.broadcasted_iota(jnp.int32, row.shape, 0)
    before = jnp.where(column == 0, F32(0), pltpu.roll(row, 1, 0))
    after = jnp.where(column == width - 1, F32(0), pltpu.roll(row, width - 1, 0))
    return before, after


def turned(row, core, out, at):
    width, channels = row.shape
    groups = channels // (16 * NC)
    flat = jnp.transpose(row)
    for g in range(groups):
        for c in range(NC):
            start = (g * NC + c) * 16
            out[c ^ core, g, :, at] = flat[start : start + 16]


def grad_body(place, cot, fm_hbm, grad, ends, fm, cot_t, fm_v, sems, step=4):
    rows, width, channels = cot.shape
    groups = channels // (16 * NC)
    core = place[2]
    parts = rows // step
    copies = []
    for q in range(parts):
        here = pl.ds(q * step, step)
        copies.append(pltpu.make_async_copy(fm_hbm.at[here], fm.at[here], sems.at[q]))
    for copy in copies:
        copy.start()
    nothing = jnp.zeros((NC, groups, 16, width), BF16)
    cot_t[:, :, :, :width] = nothing
    cot_t[:, :, :, (rows + 1) * width :] = nothing

    def prepare(q):
        copies[q].wait()
        for r in range(q * step, (q + 1) * step):
            row = fm[r]
            before, after = moved_columns(row.astype(F32))
            here = pl.ds(r * width, width)
            fm_v[0, here] = before.astype(BF16)
            fm_v[1, here] = row
            fm_v[2, here] = after.astype(BF16)
            if r in (0, rows - 1):
                ends[int(r > 0)] = row
            turned(cot[r], core, cot_t, pl.ds((r + 1) * width, width))

    def add(q):
        for u in range(3):
            left = cot_t[:, :, :, pl.ds((q * step + 2 - u) * width, step * width)]
            left = left.reshape(channels, step * width)
            for v in range(3):
                right = fm_v[v, pl.ds(q * step * width, step * width)]
                out = jnp.dot(left, right, preferred_element_type=F32)
                out = out.reshape(NC, groups, 16, channels)
                grad[3 * u + v] = out if q == 0 else grad[3 * u + v] + out

    prepare(0)
    for q in range(parts):
        if q + 1 < parts:
            prepare(q + 1)
        add(q)


def edge_body(place, grad, ends, low, high, after, mine, theirs, turn_low, turn_high):
    del after
    taps, _, groups, _, channels = grad.shape
    width = low.shape[0]
    core = place[2]
    turned(low[...], core, turn_low, pl.ds(0, width))
    turned(high[...], core, turn_high, pl.ds(0, width))

    def put(t, value):
        for g in range(groups):
            mine[g, t] = value[0, g]
            theirs[g, t] = value[1, g].astype(BF16)

    for t in (3, 4, 5):
        put(t, grad[t])
    for turn, end, tap in ((turn_high, 1, 0), (turn_low, 0, 6)):
        whole = ends[end]
        before, after = moved_columns(whole.astype(F32))
        left = turn[...].reshape(channels, width)
        for v, right in enumerate((before.astype(BF16), whole, after.astype(BF16))):
            out = jnp.dot(left, right, preferred_element_type=F32)
            put(tap + v, grad[tap + v] + out.reshape(NC, groups, 16, channels))


def split_x_body(place, mine, got, final, final_c, own, one, two, three, both):
    both[0] = final[...]
    both[1] = final_c[...]
    x = place[0]
    for k, out in ((0, own), (1, one), (2, two), (3, three)):
        base = lax.rem(x + k, NX) * NZ
        for z in range(NZ):
            out[z] = (mine[base + z] + got[base + z].astype(F32)).astype(out.dtype)


def put_row(block, row):
    at = lax.broadcasted_iota(jnp.int32, block.shape, 0)
    out = jnp.zeros(block.shape, F32)
    for n in range(3):
        part = row.astype(BF16).astype(F32)
        out = jnp.where(at == n, part, out)
        row = row - part
    block[...] = out.astype(BF16)


def take_row(block):
    rows = block[...].astype(F32)
    return (rows[0:1] + rows[1:2]) + rows[2:3]


def split_z_body(place, style, mine, one, two, three, near, got, total, other):
    taps, outs, channels = total.shape
    z = place[1]
    share = jnp.zeros((outs, channels), F32)
    for k, source in enumerate((near, got)):
        at = z ^ k
        dot = jnp.zeros((outs, channels), F32)
        values = []
        for t in range(taps):
            value = mine[at, t] + one[at, t].astype(F32) + two[at, t].astype(F32) + three[at, t].astype(F32)
            if k == 0:
                total[t] = value
            else:
                other[t] = value.astype(BF16)
            dot = dot + value * source[0, t].astype(F32)
            values.append(value)
        dot = jnp.sum(dot, axis=1, keepdims=True)
        for t in range(taps):
            final = source[0, t].astype(F32)
            share = share + (values[t] - final * dot) * final
    put_row(other.at[taps], jnp.sum(share, axis=0, keepdims=True) / style[...])


def owner_body(sel, style, kernel, total, sent, got, message, style_row):
    taps, outs, channels = kernel.shape
    top = sel.shape[1]
    s = style[...]
    style_row[...] = jnp.broadcast_to(take_row(sent.at[taps]) + take_row(got.at[taps]), style_row.shape)
    demod = demod_of(kernel, s)
    dot = jnp.zeros((outs, channels), F32)
    for t in range(taps):
        grad = total[t] + got[t].astype(F32)
        dot = dot + grad * (kernel[t] * s)
    curvature = jnp.sum(dot, axis=1, keepdims=True)
    slope = demod * demod * demod * curvature
    for t in range(taps):
        grad = total[t] + got[t].astype(F32)
        modded_grad = demod * grad - slope * (kernel[t] * s)
        message[t] = (modded_grad * s).astype(BF16)
    bank = lax.broadcasted_iota(jnp.int32, (outs, channels), 0)
    rank = jnp.zeros((outs, channels), F32)
    for j in range(top):
        rank = rank + jnp.where(bank == sel[0, j], F32(top - j), F32(0))
    message[taps] = rank.astype(BF16)


def four_body(style_row, near, got, four):
    taps = near.shape[1]
    for k, source in enumerate((near, got)):
        for c in range(NC):
            four[pl.ds((k * NC + c) * taps, taps)] = source[c]
    put_row(four.at[NZ * NC * taps], style_row[0:1])


def style_body(zero, one, two, three, out):
    last = zero.shape[0] - 1
    even = take_row(zero.at[last]) + take_row(two.at[last])
    odd = take_row(one.at[last]) + take_row(three.at[last])
    out[...] = jnp.broadcast_to(even + odd, out.shape)


def ahead_body(*refs):
    out = refs[-1]
    for k, piece in enumerate(refs[:-1]):
        out[k] = piece[...]


def banks_body(*refs):
    out, both, sems = refs[-3:]
    banks, taps, outs, channels = out.shape
    pieces = []
    for ref in refs[:-3]:
        if len(ref.shape) == 3:
            pieces.append(ref)
        else:
            pieces.extend(ref.at[n] for n in range(ref.shape[0]))
    lane = lax.broadcasted_iota(jnp.int32, (outs, channels), 1)
    row = lax.broadcasted_iota(jnp.int32, (outs, channels), 0)
    ranks = jnp.zeros((outs, channels), F32)
    for n, piece in enumerate(pieces):
        ranks = jnp.where(lane // outs == n, piece[taps].astype(F32), ranks)
    left = jnp.concatenate(
        [jnp.where(lane % outs == row, ranks[k : k + 1], F32(0)) for k in range(banks)], axis=0
    ).astype(BF16)
    copies = []
    for t in range(taps):
        right = jnp.concatenate([piece[t] for piece in pieces], axis=0)
        total = jnp.dot(left, right, preferred_element_type=F32) / F32(6)
        both[:, t] = total.reshape(banks, outs, channels)
        copy = pltpu.make_async_copy(both.at[:, t], out.at[:, t], sems.at[t])
        copy.start()
        copies.append(copy)
    for copy in copies:
        copy.wait()


def input_body(place, *refs):
    finals = refs[:NX]
    low, high, cot, after, out, final, padded, sem = refs[NX:]
    del after
    rows, width, channels = out.shape
    copy = pltpu.make_async_copy(cot, padded.at[pl.ds(1, rows)], sem)
    copy.start()
    padded[0] = low[...]
    padded[rows + 1] = high[...]
    x, z, core = place[0], place[1], place[2]
    for k in range(NX):
        for n in range(NZ):
            for c in range(NC):
                at = (lax.rem(x + NX - k, NX) * NZ + (z ^ n)) * NC + (core ^ c)
                here = pl.ds(pl.multiple_of(at * 16, 16), 16)
                for t in range(9):
                    u, v = t // 3, t % 3
                    final[u, here, v * channels : (v + 1) * channels] = finals[k][(n * NC + c) * 9 + t]
    copy.wait()
    step = 2

    @pl.loop(0, rows // step)
    def _(q):
        r = q * step
        left = jnp.concatenate(
            [padded[pl.ds(r + 2 - u, step)].reshape(step * width, channels) for u in range(3)], axis=1
        )
        right = final[...].reshape(3 * channels, 3 * channels)
        sums = jnp.dot(left, right, preferred_element_type=F32)
        for n in range(step):
            part = sums[n * width : (n + 1) * width]
            _, after = moved_columns(part[:, :channels])
            before, _ = moved_columns(part[:, 2 * channels :])
            out[r + n] = (part[:, channels : 2 * channels] + after + before).astype(BF16)


def local(feature_map, cotangent, style, bank, selection):
    _, rows, width, channels = feature_map.shape
    fm = feature_map.reshape(rows, width, channels)
    cot = cotangent.reshape(rows, width, channels)
    banks, own_out, taps, _ = bank.shape
    groups = NX * NZ
    tile = lax.axis_index("tile")
    place = jnp.stack([tile // (NZ * NC), (tile // NC) % NZ, tile % NC]).astype(jnp.int32)
    dma = pltpu.SemaphoreType.DMA
    piece = (taps, own_out, channels)
    pair = (NZ,) + piece
    message_of = (taps + 1, own_out, channels)

    last, first = call(
        rows_body, (shape((width, channels), BF16),) * 2, [HBM], [dma((2, 4))], nbytes=10**6, vmem=60 << 20, name="rows"
    )(cot)
    count = lax.axis_size("tile")
    low = lax.ppermute(last, "tile", [(i, i + 1) for i in range(count - 1)])
    high = lax.ppermute(first, "tile", [(i + 1, i) for i in range(count - 1)])

    kernel, final = call(
        mix_body, (shape(piece, F32), shape(piece, BF16)), [SMEM, VMEM, VMEM], flops=10**6, nbytes=10**6, name="mix"
    )(selection, style, jnp.transpose(bank, (0, 2, 1, 3)))
    final_c = swap_core(final)

    grad, ends = call(
        grad_body,
        (shape((taps, NC, groups, 16, channels), F32), shape((2, width, channels), BF16)),
        [SMEM, VMEM, HBM],
        [
            pltpu.VMEM((rows, width, channels), BF16),
            pltpu.VMEM((NC, groups, 16, (rows + 2) * width), BF16),
            pltpu.VMEM((3, rows * width, channels), BF16),
            dma((4,)),
        ],
        flops=2 * 9 * rows * width * channels * channels,
        nbytes=4 * rows * width * channels,
        vmem=50 << 20,
        name="grad",
    )(place, cot, fm)
    mine, theirs = call(
        edge_body,
        (shape((groups,) + piece, F32), shape((groups,) + piece, BF16)),
        [SMEM] + [VMEM] * 5,
        [pltpu.VMEM((NC, groups, 16, width), BF16)] * 2,
        flops=2 * 6 * width * channels * channels,
        nbytes=4 * 10**6,
        vmem=50 << 20,
        name="edge",
    )(place, grad, ends, low, high, final_c)

    own_x, one, two, three, both = call(
        split_x_body,
        (shape(pair, F32),) + (shape(pair, BF16),) * 3 + (shape((NC,) + piece, BF16),),
        [SMEM] + [VMEM] * 4,
        flops=10**6,
        nbytes=3 * 10**6,
        name="split_x",
    )(place, mine, swap_core(theirs), final, final_c)
    got_z = swap_z(both)
    total, other = call(
        split_z_body,
        (shape(piece, F32), shape(message_of, BF16)),
        [SMEM] + [VMEM] * 7,
        flops=10**6,
        nbytes=10**6,
        name="split_z",
    )(place, style, own_x, shift_x(one, 1), shift_x(two, 2), shift_x(three, 3), both, got_z)
    message, style_row = call(
        owner_body,
        (shape(message_of, BF16), shape((8, channels), F32)),
        [SMEM] + [VMEM] * 5,
        flops=10**6,
        nbytes=10**6,
        name="owner",
    )(selection, style, kernel, total, other, swap_z(other))

    four = call(
        four_body,
        shape((NZ * NC * taps + 1, own_out, channels), BF16),
        [VMEM] * 3,
        flops=10**9,
        nbytes=10**7,
        name="four",
    )(style_row, both, got_z)
    finals = [four] + [shift_x(four, k) for k in range(1, NX)]
    style_part = call(style_body, shape((8, channels), F32), [VMEM] * NX, name="style")(*finals)
    style_sum = style_part + swap_core(style_part)

    over_l = [flip_l(message, k) for k in range(1, NL)]
    ahead = call(ahead_body, shape((NL,) + message_of, BF16), [VMEM] * NL, name="ahead")(message, *over_l)
    over_y = [shift_y(ahead, k) for k in range(1, NY)]

    input_grad = call(
        input_body,
        shape((rows, width, channels), BF16),
        [SMEM] + [VMEM] * (NX + 2) + [HBM, VMEM],
        [
            pltpu.VMEM((3, channels, 3 * channels), BF16),
            pltpu.VMEM((rows + 2, width, channels), BF16),
            dma,
        ],
        flops=2 * 9 * rows * width * channels * channels,
        nbytes=4 * rows * width * channels,
        vmem=50 << 20,
        name="input",
    )(place, *finals, low, high, cot, ahead)

    bank_grad = pl.pallas_call(
        banks_body,
        out_shape=shape((banks,) + piece, F32),
        in_specs=[VMEM] * NY,
        out_specs=HBM,
        scratch_shapes=[pltpu.VMEM((banks,) + piece, F32), dma((taps,))],
        compiler_params=pltpu.CompilerParams(vmem_limit_bytes=16 << 20),
        cost_estimate=pl.CostEstimate(flops=10**7, bytes_accessed=3 * 10**6, transcendentals=0),
        name="banks",
    )(ahead, *over_y)

    return (
        input_grad.reshape(feature_map.shape),
        style_sum[:1],
        jnp.transpose(bank_grad, (0, 2, 1, 3)),
    )


def solution(mesh):
    in_specs = (
        P("img", "tile", None, None),
        P("img", "tile", None, None),
        P("img", None),
        P(None, "tile", None, None),
        P("img", None),
    )
    out_specs = (P("img", "tile", None, None), P("img", None), P(None, "tile", None, None))
    return jax.shard_map(local, mesh=mesh, in_specs=in_specs, out_specs=out_specs, check_vma=False)
```

```python
import functools

import jax
import jax.numpy as jnp
from jax import lax
from jax.experimental import pallas as pl
from jax.experimental.pallas import tpu as pltpu
from jax.sharding import PartitionSpec as P

epsilon = 1e-06
F32 = jnp.float32
BF16 = jnp.bfloat16
VMEM = pl.BlockSpec(memory_space=pltpu.VMEM)
SMEM = pl.BlockSpec(memory_space=pltpu.SMEM)
ANY = pl.BlockSpec(memory_space=pl.ANY)
HBM = pl.BlockSpec(memory_space=pltpu.HBM)

NX, NZ, NC = 4, 2, 2
NL, NY = 4, 4


def tile_perm(move):
    place = lambda x, z, c: (x * NZ + z) * NC + c
    return [
        (place(x, z, c), place(*move(x, z, c)))
        for x in range(NX)
        for z in range(NZ)
        for c in range(NC)
    ]


def img_perm(move):
    place = lambda l, y: l * NY + y
    return [(place(l, y), place(*move(l, y))) for l in range(NL) for y in range(NY)]


def swap_core(a):
    return lax.ppermute(a, "tile", tile_perm(lambda x, z, c: (x, z, 1 - c)))


def swap_z(a):
    return lax.ppermute(a, "tile", tile_perm(lambda x, z, c: (x, 1 - z, c)))


def shift_x(a, k):
    return lax.ppermute(a, "tile", tile_perm(lambda x, z, c: ((x + k) % NX, z, c)))


def flip_x(a, k):
    return lax.ppermute(a, "tile", tile_perm(lambda x, z, c: (x ^ k, z, c)))


def flip_l(a, k):
    return lax.ppermute(a, "img", img_perm(lambda l, y: (l ^ k, y)))


def shift_y(a, k):
    return lax.ppermute(a, "img", img_perm(lambda l, y: (l, (y + k) % NY)))


def call(body, outs, in_specs, scratch=(), flops=0, nbytes=0, vmem=16 << 20, out=VMEM, name=None):
    return pl.pallas_call(
        body,
        out_shape=outs,
        in_specs=in_specs,
        out_specs=jax.tree.map(lambda _: out, outs),
        scratch_shapes=list(scratch),
        compiler_params=pltpu.CompilerParams(vmem_limit_bytes=vmem),
        cost_estimate=pl.CostEstimate(flops=flops, bytes_accessed=nbytes, transcendentals=0),
        name=name,
    )


def shape(s, dtype):
    return jax.ShapeDtypeStruct(s, dtype)


def demod_of(kernel, style):
    total = None
    for t in range(kernel.shape[0]):
        modded = kernel[t] * style
        total = modded * modded if total is None else total + modded * modded
    return lax.rsqrt(jnp.sum(total, axis=1, keepdims=True) + epsilon)


def fetch(copies):
    for copy in copies:
        copy.start()
    for copy in copies:
        copy.wait()


def rows_body(cot, last, first, sems):
    rows, width = cot.shape[:2]
    parts = sems.shape[1]
    copies = []
    for n, (row, out) in enumerate(((rows - 1, last), (0, first))):
        for p in range(parts):
            here = pl.ds(p * (width // parts), width // parts)
            copies.append(pltpu.make_async_copy(cot.at[row, here], out.at[here], sems.at[n, p]))
    fetch(copies)


def mix_body(sel, style, bank, kernel, final):
    banks, taps = bank.shape[:2]
    top = sel.shape[1]
    weights = []
    for k in range(banks):
        w = F32(0)
        for j in range(top):
            w = w + jnp.where(sel[0, j] == k, F32((top - j) / (top * (top + 1) / 2)), F32(0))
        weights.append(w)
    for t in range(taps):
        mixed = None
        for k in range(banks):
            term = weights[k] * bank[k, t].astype(F32)
            mixed = term if mixed is None else mixed + term
        kernel[t] = mixed
    demod = demod_of(kernel, style[...])
    for t in range(taps):
        final[t] = (kernel[t] * style[...] * demod).astype(BF16)


def moved_columns(row):
    width = row.shape[0]
    column = lax.broadcasted_iota(jnp.int32, row.shape, 0)
    before = jnp.where(column == 0, F32(0), pltpu.roll(row, 1, 0))
    after = jnp.where(column == width - 1, F32(0), pltpu.roll(row, width - 1, 0))
    return before, after


def turned(row, core, out, at):
    width, channels = row.shape
    groups = channels // (16 * NC)
    flat = jnp.transpose(row)
    for g in range(groups):
        for c in range(NC):
            start = (g * NC + c) * 16
            out[c ^ core, g, :, at] = flat[start : start + 16]


def grad_body(place, cot, fm, grad, ends, cot_t, fm_v, step=4):
    rows, width, channels = cot.shape
    groups = channels // (16 * NC)
    core = place[2]
    parts = rows // step
    nothing = jnp.zeros((NC, groups, 16, width), BF16)
    cot_t[:, :, :, :width] = nothing
    cot_t[:, :, :, (rows + 1) * width :] = nothing

    def prepare(q):
        for r in range(q * step, (q + 1) * step):
            row = fm[r]
            before, after = moved_columns(row.astype(F32))
            here = pl.ds(r * width, width)
            fm_v[0, here] = before.astype(BF16)
            fm_v[1, here] = row
            fm_v[2, here] = after.astype(BF16)
            if r in (0, rows - 1):
                ends[int(r > 0)] = row
            turned(cot[r], core, cot_t, pl.ds((r + 1) * width, width))

    def add(q):
        for u in range(3):
            left = cot_t[:, :, :, pl.ds((q * step + 2 - u) * width, step * width)]
            left = left.reshape(channels, step * width)
            for v in range(3):
                right = fm_v[v, pl.ds(q * step * width, step * width)]
                out = jnp.dot(left, right, preferred_element_type=F32)
                out = out.reshape(NC, groups, 16, channels)
                grad[3 * u + v] = out if q == 0 else grad[3 * u + v] + out

    prepare(0)
    for q in range(parts):
        if q + 1 < parts:
            prepare(q + 1)
        add(q)


def edge_body(place, grad, ends, low, high, after, mine, theirs, turn_low, turn_high):
    del after
    taps, _, groups, _, channels = grad.shape
    width = low.shape[0]
    core = place[2]
    turned(low[...], core, turn_low, pl.ds(0, width))
    turned(high[...], core, turn_high, pl.ds(0, width))

    def put(t, value):
        for g in range(groups):
            mine[g, t] = value[0, g]
            theirs[g, t] = value[1, g].astype(BF16)

    for t in (3, 4, 5):
        put(t, grad[t])
    for turn, end, tap in ((turn_high, 1, 0), (turn_low, 0, 6)):
        whole = ends[end]
        before, after = moved_columns(whole.astype(F32))
        left = turn[...].reshape(channels, width)
        for v, right in enumerate((before.astype(BF16), whole, after.astype(BF16))):
            out = jnp.dot(left, right, preferred_element_type=F32)
            put(tap + v, grad[tap + v] + out.reshape(NC, groups, 16, channels))


def split_x_body(place, mine, got, own, one, two, three):
    x = place[0]
    for k, out in ((0, own), (1, one), (2, two), (3, three)):
        base = lax.rem(x + k, NX) * NZ
        for z in range(NZ):
            out[z] = (mine[base + z] + got[base + z].astype(F32)).astype(out.dtype)


def put_row(block, row):
    at = lax.broadcasted_iota(jnp.int32, block.shape, 0)
    out = jnp.zeros(block.shape, F32)
    for n in range(3):
        part = row.astype(BF16).astype(F32)
        out = jnp.where(at == n, part, out)
        row = row - part
    block[...] = out.astype(BF16)


def take_row(block):
    rows = block[...].astype(F32)
    return (rows[0:1] + rows[1:2]) + rows[2:3]


def split_z_body(place, style, mine, one, two, three, near, got, after, after_too, total, other):
    del after, after_too
    taps, outs, channels = total.shape
    z = place[1]
    share = jnp.zeros((outs, channels), F32)
    for k, source in enumerate((near, got)):
        at = z ^ k
        dot = jnp.zeros((outs, channels), F32)
        values = []
        for t in range(taps):
            value = mine[at, t] + one[at, t].astype(F32) + two[at, t].astype(F32) + three[at, t].astype(F32)
            if k == 0:
                total[t] = value
            else:
                other[t] = value.astype(BF16)
            dot = dot + value * source[t].astype(F32)
            values.append(value)
        dot = jnp.sum(dot, axis=1, keepdims=True)
        for t in range(taps):
            final = source[t].astype(F32)
            share = share + (values[t] - final * dot) * final
    put_row(other.at[taps], jnp.sum(share, axis=0, keepdims=True) / style[...])


def owner_body(sel, style, kernel, total, sent, got, message, style_row):
    taps, outs, channels = kernel.shape
    top = sel.shape[1]
    s = style[...]
    style_row[...] = jnp.broadcast_to(take_row(sent.at[taps]) + take_row(got.at[taps]), style_row.shape)
    demod = demod_of(kernel, s)
    dot = jnp.zeros((outs, channels), F32)
    for t in range(taps):
        grad = total[t] + got[t].astype(F32)
        dot = dot + grad * (kernel[t] * s)
    curvature = jnp.sum(dot, axis=1, keepdims=True)
    slope = demod * demod * demod * curvature
    for t in range(taps):
        grad = total[t] + got[t].astype(F32)
        modded_grad = demod * grad - slope * (kernel[t] * s)
        message[t] = (modded_grad * s).astype(BF16)
    bank = lax.broadcasted_iota(jnp.int32, (outs, channels), 0)
    rank = jnp.zeros((outs, channels), F32)
    for j in range(top):
        rank = rank + jnp.where(bank == sel[0, j], F32(top - j), F32(0))
    message[taps] = rank.astype(BF16)


def kernels_body(style_row, *refs):
    out = refs[-1]
    taps = refs[0].shape[0]
    for n, piece in enumerate(refs[:-1]):
        out[pl.ds(n * taps, taps)] = piece[...]
    put_row(out.at[(len(refs) - 1) * taps], style_row[0:1])


def style_body(*refs):
    out = refs[-1]
    zero, one, two, three = [take_row(ref.at[ref.shape[0] - 1]) for ref in refs[:-1]]
    out[...] = jnp.broadcast_to((zero + two) + (one + three), out.shape)


def ahead_body(*refs):
    out = refs[-1]
    for k, piece in enumerate(refs[:-1]):
        out[k] = piece[...]


def banks_body(*refs):
    out, both, sems = refs[-3:]
    banks, taps, outs, channels = out.shape
    pieces = []
    for ref in refs[:-3]:
        if len(ref.shape) == 3:
            pieces.append(ref)
        else:
            pieces.extend(ref.at[n] for n in range(ref.shape[0]))
    lane = lax.broadcasted_iota(jnp.int32, (outs, channels), 1)
    row = lax.broadcasted_iota(jnp.int32, (outs, channels), 0)
    ranks = jnp.zeros((outs, channels), F32)
    for n, piece in enumerate(pieces):
        ranks = jnp.where(lane // outs == n, piece[taps].astype(F32), ranks)
    left = jnp.concatenate(
        [jnp.where(lane % outs == row, ranks[k : k + 1], F32(0)) for k in range(banks)], axis=0
    ).astype(BF16)
    copies = []
    for t in range(taps):
        right = jnp.concatenate([piece[t] for piece in pieces], axis=0)
        total = jnp.dot(left, right, preferred_element_type=F32) / F32(6)
        both[:, t] = total.reshape(banks, outs, channels)
        copy = pltpu.make_async_copy(both.at[:, t], out.at[:, t], sems.at[t])
        copy.start()
        copies.append(copy)
    for copy in copies:
        copy.wait()


def input_body(place, *refs, step=2):
    finals = refs[:NX]
    low, high, cot, after, out, final, done, sems = refs[NX:]
    del after
    rows, width, channels = cot.shape
    x, z, core = place[0], place[1], place[2]
    for k in range(NX):
        for n in range(NZ):
            for c in range(NC):
                at = (lax.rem(x + NX - k, NX) * NZ + (z ^ n)) * NC + (core ^ c)
                here = pl.ds(pl.multiple_of(at * 16, 16), 16)
                for t in range(9):
                    u, v = t // 3, t % 3
                    final[u, here, v * channels : (v + 1) * channels] = finals[k][(n * NC + c) * 9 + t]

    def part(start):
        if start < 0:
            return jnp.concatenate([low[...], cot[0 : step - 1].reshape((step - 1) * width, channels)], axis=0)
        if start + step > rows:
            return jnp.concatenate([cot[start:rows].reshape((rows - start) * width, channels), high[...]], axis=0)
        return cot[start : start + step].reshape(step * width, channels)

    copies = []
    for q in range(rows // step):
        r = q * step
        left = jnp.concatenate([part(r + 1 - u) for u in range(3)], axis=1)
        right = final[...].reshape(3 * channels, 3 * channels)
        sums = jnp.dot(left, right, preferred_element_type=F32)
        for n in range(step):
            piece = sums[n * width : (n + 1) * width]
            _, after = moved_columns(piece[:, :channels])
            before, _ = moved_columns(piece[:, 2 * channels :])
            done[q * step + n] = (piece[:, channels : 2 * channels] + after + before).astype(BF16)
        copy = pltpu.make_async_copy(done.at[pl.ds(q * step, step)], out.at[pl.ds(r, step)], sems.at[q])
        copy.start()
        copies.append(copy)
    for copy in copies:
        copy.wait()


def local(feature_map, cotangent, style, bank, selection):
    _, rows, width, channels = feature_map.shape
    fm = feature_map.reshape(rows, width, channels)
    cot = cotangent.reshape(rows, width, channels)
    banks, own_out, taps, _ = bank.shape
    groups = NX * NZ
    tile = lax.axis_index("tile")
    place = jnp.stack([tile // (NZ * NC), (tile // NC) % NZ, tile % NC]).astype(jnp.int32)
    dma = pltpu.SemaphoreType.DMA
    piece = (taps, own_out, channels)
    pair = (NZ,) + piece
    message_of = (taps + 1, own_out, channels)

    last, first = call(
        rows_body,
        (shape((width, channels), BF16),) * 2,
        [HBM],
        [dma((2, 2))],
        nbytes=10**6,
        vmem=60 << 20,
        out=HBM,
        name="rows",
    )(cot)
    count = lax.axis_size("tile")
    low = lax.ppermute(last, "tile", [(i, i + 1) for i in range(count - 1)])
    high = lax.ppermute(first, "tile", [(i + 1, i) for i in range(count - 1)])

    kernel, final = call(
        mix_body, (shape(piece, F32), shape(piece, BF16)), [SMEM, VMEM, VMEM], flops=10**6, nbytes=10**6, name="mix"
    )(selection, style, jnp.transpose(bank, (0, 2, 1, 3)))
    final_z = swap_z(final)
    final_c = swap_core(final)
    final_cz = swap_core(final_z)

    grad, ends = call(
        grad_body,
        (shape((taps, NC, groups, 16, channels), F32), shape((2, width, channels), BF16)),
        [SMEM, VMEM, VMEM],
        [
            pltpu.VMEM((NC, groups, 16, (rows + 2) * width), BF16),
            pltpu.VMEM((3, rows * width, channels), BF16),
        ],
        flops=2 * 9 * rows * width * channels * channels,
        nbytes=4 * rows * width * channels,
        vmem=24 << 20,
        name="grad",
    )(place, cot, fm)
    mine, theirs = call(
        edge_body,
        (shape((groups,) + piece, F32), shape((groups,) + piece, BF16)),
        [SMEM] + [VMEM] * 5,
        [pltpu.VMEM((NC, groups, 16, width), BF16)] * 2,
        flops=2 * 6 * width * channels * channels,
        nbytes=4 * 10**6,
        name="edge",
    )(place, grad, ends, low, high, final_z)

    own_x, one, two, three = call(
        split_x_body,
        (shape(pair, F32),) + (shape(pair, BF16),) * 3,
        [SMEM] + [VMEM] * 2,
        flops=10**6,
        nbytes=3 * 10**6,
        name="split_x",
    )(place, mine, swap_core(theirs))
    total, other = call(
        split_z_body,
        (shape(piece, F32), shape(message_of, BF16)),
        [SMEM] + [VMEM] * 9,
        flops=10**6,
        nbytes=10**6,
        name="split_z",
    )(place, style, own_x, shift_x(one, 1), shift_x(two, 2), shift_x(three, 3), final, final_z, final_c, final_cz)
    message, style_row = call(
        owner_body,
        (shape(message_of, BF16), shape((8, channels), F32)),
        [SMEM] + [VMEM] * 5,
        flops=10**6,
        nbytes=10**6,
        name="owner",
    )(selection, style, kernel, total, other, swap_z(other))

    kernels = call(
        kernels_body,
        shape((NZ * NC * taps + 1, own_out, channels), BF16),
        [VMEM] * 5,
        flops=10**9,
        nbytes=10**7,
        name="kernels",
    )(style_row, final, final_c, final_z, final_cz)
    finals = [kernels] + [shift_x(kernels, k) for k in range(1, NX)]
    style_part = call(style_body, shape((8, channels), F32), [VMEM] * NX, name="style")(*finals)
    style_sum = style_part + swap_core(style_part)

    over_l = [flip_l(message, k) for k in range(1, NL)]
    ahead = call(ahead_body, shape((NL,) + message_of, BF16), [VMEM] * NL, name="ahead")(message, *over_l)
    over_y = [shift_y(ahead, k) for k in range(1, NY)]

    input_grad = call(
        input_body,
        shape((rows, width, channels), BF16),
        [SMEM] + [VMEM] * (NX + 4),
        [
            pltpu.VMEM((3, channels, 3 * channels), BF16),
            pltpu.VMEM((rows, width, channels), BF16),
            dma((8,)),
        ],
        flops=2 * 9 * rows * width * channels * channels,
        nbytes=4 * rows * width * channels,
        vmem=24 << 20,
        out=HBM,
        name="input",
    )(place, *finals, low, high, cot, ahead)

    bank_grad = pl.pallas_call(
        banks_body,
        out_shape=shape((banks,) + piece, F32),
        in_specs=[VMEM] * NY,
        out_specs=HBM,
        scratch_shapes=[pltpu.VMEM((banks,) + piece, F32), dma((taps,))],
        compiler_params=pltpu.CompilerParams(vmem_limit_bytes=16 << 20),
        cost_estimate=pl.CostEstimate(flops=10**7, bytes_accessed=3 * 10**6, transcendentals=0),
        name="banks",
    )(ahead, *over_y)

    return (
        input_grad.reshape(feature_map.shape),
        style_sum[:1],
        jnp.transpose(bank_grad, (0, 2, 1, 3)),
    )


def solution(mesh):
    in_specs = (
        P("img", "tile", None, None),
        P("img", "tile", None, None),
        P("img", None),
        P(None, "tile", None, None),
        P("img", None),
    )
    out_specs = (P("img", "tile", None, None), P("img", None), P(None, "tile", None, None))
    return jax.shard_map(local, mesh=mesh, in_specs=in_specs, out_specs=out_specs, check_vma=False)
```

```python
import functools

import jax
import jax.numpy as jnp
from jax import lax
from jax.experimental import pallas as pl
from jax.experimental.pallas import tpu as pltpu
from jax.sharding import PartitionSpec as P

epsilon = 1e-06
F32 = jnp.float32
BF16 = jnp.bfloat16
VMEM = pl.BlockSpec(memory_space=pltpu.VMEM)
SMEM = pl.BlockSpec(memory_space=pltpu.SMEM)
ANY = pl.BlockSpec(memory_space=pl.ANY)
HBM = pl.BlockSpec(memory_space=pltpu.HBM)

NX, NZ, NC = 4, 2, 2
NL, NY = 4, 4


def tile_perm(move):
    place = lambda x, z, c: (x * NZ + z) * NC + c
    return [
        (place(x, z, c), place(*move(x, z, c)))
        for x in range(NX)
        for z in range(NZ)
        for c in range(NC)
    ]


def img_perm(move):
    place = lambda l, y: l * NY + y
    return [(place(l, y), place(*move(l, y))) for l in range(NL) for y in range(NY)]


def swap_core(a):
    return lax.ppermute(a, "tile", tile_perm(lambda x, z, c: (x, z, 1 - c)))


def swap_z(a):
    return lax.ppermute(a, "tile", tile_perm(lambda x, z, c: (x, 1 - z, c)))


def shift_x(a, k):
    return lax.ppermute(a, "tile", tile_perm(lambda x, z, c: ((x + k) % NX, z, c)))


def flip_x(a, k):
    return lax.ppermute(a, "tile", tile_perm(lambda x, z, c: (x ^ k, z, c)))


def flip_l(a, k):
    return lax.ppermute(a, "img", img_perm(lambda l, y: (l ^ k, y)))


def shift_y(a, k):
    return lax.ppermute(a, "img", img_perm(lambda l, y: (l, (y + k) % NY)))


def call(body, outs, in_specs, scratch=(), flops=0, nbytes=0, vmem=16 << 20, out=VMEM, name=None):
    return pl.pallas_call(
        body,
        out_shape=outs,
        in_specs=in_specs,
        out_specs=out if isinstance(out, tuple) else jax.tree.map(lambda _: out, outs),
        scratch_shapes=list(scratch),
        compiler_params=pltpu.CompilerParams(vmem_limit_bytes=vmem),
        cost_estimate=pl.CostEstimate(flops=flops, bytes_accessed=nbytes, transcendentals=0),
        name=name,
    )


def shape(s, dtype):
    return jax.ShapeDtypeStruct(s, dtype)


def demod_of(kernel, style):
    total = None
    for t in range(kernel.shape[0]):
        modded = kernel[t] * style
        total = modded * modded if total is None else total + modded * modded
    return lax.rsqrt(jnp.sum(total, axis=1, keepdims=True) + epsilon)


def fetch(copies):
    for copy in copies:
        copy.start()
    for copy in copies:
        copy.wait()


def rows_body(cot, last, first, sems):
    rows, width = cot.shape[:2]
    parts = sems.shape[1]
    copies = []
    for n, (row, out) in enumerate(((rows - 1, last), (0, first))):
        for p in range(parts):
            here = pl.ds(p * (width // parts), width // parts)
            copies.append(pltpu.make_async_copy(cot.at[row, here], out.at[here], sems.at[n, p]))
    fetch(copies)


def mix_body(sel, style, bank, kernel, final):
    banks, taps = bank.shape[:2]
    top = sel.shape[1]
    weights = []
    for k in range(banks):
        w = F32(0)
        for j in range(top):
            w = w + jnp.where(sel[0, j] == k, F32((top - j) / (top * (top + 1) / 2)), F32(0))
        weights.append(w)
    for t in range(taps):
        mixed = None
        for k in range(banks):
            term = weights[k] * bank[k, t].astype(F32)
            mixed = term if mixed is None else mixed + term
        kernel[t] = mixed
    demod = demod_of(kernel, style[...])
    for t in range(taps):
        final[t] = (kernel[t] * style[...] * demod).astype(BF16)


def moved_columns(row):
    width = row.shape[0]
    column = lax.broadcasted_iota(jnp.int32, row.shape, 0)
    before = jnp.where(column == 0, F32(0), pltpu.roll(row, 1, 0))
    after = jnp.where(column == width - 1, F32(0), pltpu.roll(row, width - 1, 0))
    return before, after


def turned(row, core, out, at):
    width, channels = row.shape
    groups = channels // (16 * NC)
    flat = jnp.transpose(row)
    for g in range(groups):
        for c in range(NC):
            start = (g * NC + c) * 16
            out[c ^ core, g, :, at] = flat[start : start + 16]


def grad_body(place, cot, fm, grad, ends, cot_t, fm_v, step=4):
    rows, width, channels = cot.shape
    groups = channels // (16 * NC)
    core = place[2]
    parts = rows // step
    nothing = jnp.zeros((NC, groups, 16, width), BF16)
    cot_t[:, :, :, :width] = nothing
    cot_t[:, :, :, (rows + 1) * width :] = nothing

    def prepare(q):
        for r in range(q * step, (q + 1) * step):
            row = fm[r]
            before, after = moved_columns(row.astype(F32))
            here = pl.ds(r * width, width)
            fm_v[0, here] = before.astype(BF16)
            fm_v[1, here] = row
            fm_v[2, here] = after.astype(BF16)
            if r in (0, rows - 1):
                ends[int(r > 0)] = row
            turned(cot[r], core, cot_t, pl.ds((r + 1) * width, width))

    def add(q):
        for u in range(3):
            left = cot_t[:, :, :, pl.ds((q * step + 2 - u) * width, step * width)]
            left = left.reshape(channels, step * width)
            for v in range(3):
                right = fm_v[v, pl.ds(q * step * width, step * width)]
                out = jnp.dot(left, right, preferred_element_type=F32)
                out = out.reshape(NC, groups, 16, channels)
                grad[3 * u + v] = out if q == 0 else grad[3 * u + v] + out

    prepare(0)
    for q in range(parts):
        if q + 1 < parts:
            prepare(q + 1)
        add(q)


def edge_body(place, grad, ends, low, high, after, mine, theirs, turn_low, turn_high):
    del after
    taps, _, groups, _, channels = grad.shape
    width = low.shape[0]
    core = place[2]
    turned(low[...], core, turn_low, pl.ds(0, width))
    turned(high[...], core, turn_high, pl.ds(0, width))

    def put(t, value):
        for g in range(groups):
            mine[g, t] = value[0, g]
            theirs[g, t] = value[1, g].astype(BF16)

    for t in (3, 4, 5):
        put(t, grad[t])
    for turn, end, tap in ((turn_high, 1, 0), (turn_low, 0, 6)):
        whole = ends[end]
        before, after = moved_columns(whole.astype(F32))
        left = turn[...].reshape(channels, width)
        for v, right in enumerate((before.astype(BF16), whole, after.astype(BF16))):
            out = jnp.dot(left, right, preferred_element_type=F32)
            put(tap + v, grad[tap + v] + out.reshape(NC, groups, 16, channels))


def split_x_body(place, mine, got, own, one, two, three):
    x = place[0]
    for k, out in ((0, own), (1, one), (2, two), (3, three)):
        base = lax.rem(x + k, NX) * NZ
        for z in range(NZ):
            out[z] = (mine[base + z] + got[base + z].astype(F32)).astype(out.dtype)


def put_row(block, row):
    at = lax.broadcasted_iota(jnp.int32, block.shape, 0)
    out = jnp.zeros(block.shape, F32)
    for n in range(3):
        part = row.astype(BF16).astype(F32)
        out = jnp.where(at == n, part, out)
        row = row - part
    block[...] = out.astype(BF16)


def take_row(block):
    rows = block[...].astype(F32)
    return (rows[0:1] + rows[1:2]) + rows[2:3]


def split_z_body(place, style, mine, one, two, three, near, got, after, after_too, total, other):
    del after, after_too
    taps, outs, channels = total.shape
    z = place[1]
    share = jnp.zeros((outs, channels), F32)
    for k, source in enumerate((near, got)):
        at = z ^ k
        dot = jnp.zeros((outs, channels), F32)
        values = []
        for t in range(taps):
            value = mine[at, t] + one[at, t].astype(F32) + two[at, t].astype(F32) + three[at, t].astype(F32)
            if k == 0:
                total[t] = value
            else:
                other[t] = value.astype(BF16)
            dot = dot + value * source[t].astype(F32)
            values.append(value)
        dot = jnp.sum(dot, axis=1, keepdims=True)
        for t in range(taps):
            final = source[t].astype(F32)
            share = share + (values[t] - final * dot) * final
    put_row(other.at[taps], jnp.sum(share, axis=0, keepdims=True) / style[...])


def owner_body(sel, style, kernel, total, sent, got, message, style_row):
    taps, outs, channels = kernel.shape
    top = sel.shape[1]
    s = style[...]
    style_row[...] = jnp.broadcast_to(take_row(sent.at[taps]) + take_row(got.at[taps]), style_row.shape)
    demod = demod_of(kernel, s)
    dot = jnp.zeros((outs, channels), F32)
    for t in range(taps):
        grad = total[t] + got[t].astype(F32)
        dot = dot + grad * (kernel[t] * s)
    curvature = jnp.sum(dot, axis=1, keepdims=True)
    slope = demod * demod * demod * curvature
    for t in range(taps):
        grad = total[t] + got[t].astype(F32)
        modded_grad = demod * grad - slope * (kernel[t] * s)
        message[t] = (modded_grad * s).astype(BF16)
    bank = lax.broadcasted_iota(jnp.int32, (outs, channels), 0)
    rank = jnp.zeros((outs, channels), F32)
    for j in range(top):
        rank = rank + jnp.where(bank == sel[0, j], F32(top - j), F32(0))
    message[taps] = rank.astype(BF16)


def kernels_body(style_row, *refs):
    out = refs[-1]
    taps = refs[0].shape[0]
    for n, piece in enumerate(refs[:-1]):
        out[pl.ds(n * taps, taps)] = piece[...]
    put_row(out.at[(len(refs) - 1) * taps], style_row[0:1])


def style_body(*refs):
    out = refs[-1]
    zero, one, two, three = [take_row(ref.at[ref.shape[0] - 1]) for ref in refs[:NX]]
    out[...] = jnp.broadcast_to((zero + two) + (one + three), out.shape)


def ahead_body(*refs):
    out = refs[-1]
    for k, piece in enumerate(refs[:-1]):
        out[k] = piece[...]


def banks_body(*refs):
    out, style, both, sems = refs[-4:]
    banks, taps, outs, channels = out.shape
    style[...] = refs[0][0:1] + refs[1][0:1]
    pieces = []
    for ref in refs[2:-4]:
        if len(ref.shape) == 3:
            pieces.append(ref)
        else:
            pieces.extend(ref.at[n] for n in range(ref.shape[0]))
    lane = lax.broadcasted_iota(jnp.int32, (outs, channels), 1)
    row = lax.broadcasted_iota(jnp.int32, (outs, channels), 0)
    ranks = jnp.zeros((outs, channels), F32)
    for n, piece in enumerate(pieces):
        ranks = jnp.where(lane // outs == n, piece[taps].astype(F32), ranks)
    left = jnp.concatenate(
        [jnp.where(lane % outs == row, ranks[k : k + 1], F32(0)) for k in range(banks)], axis=0
    ).astype(BF16)
    copies = []
    for t in range(taps):
        right = jnp.concatenate([piece[t] for piece in pieces], axis=0)
        total = jnp.dot(left, right, preferred_element_type=F32) / F32(6)
        both[:, t] = total.reshape(banks, outs, channels)
        copy = pltpu.make_async_copy(both.at[:, t], out.at[:, t], sems.at[t])
        copy.start()
        copies.append(copy)
    for copy in copies:
        copy.wait()


def input_body(place, *refs, step=2):
    finals = refs[:NX]
    low, high, cot, after, out, token, final, done, sems = refs[NX:]
    del after
    token[...] = jnp.zeros(token.shape, F32)
    rows, width, channels = cot.shape
    x, z, core = place[0], place[1], place[2]
    for k in range(NX):
        for n in range(NZ):
            for c in range(NC):
                at = (lax.rem(x + NX - k, NX) * NZ + (z ^ n)) * NC + (core ^ c)
                here = pl.ds(pl.multiple_of(at * 16, 16), 16)
                for t in range(9):
                    u, v = t // 3, t % 3
                    final[u, here, v * channels : (v + 1) * channels] = finals[k][(n * NC + c) * 9 + t]

    def part(start):
        if start < 0:
            return jnp.concatenate([low[...], cot[0 : step - 1].reshape((step - 1) * width, channels)], axis=0)
        if start + step > rows:
            return jnp.concatenate([cot[start:rows].reshape((rows - start) * width, channels), high[...]], axis=0)
        return cot[start : start + step].reshape(step * width, channels)

    copies = []
    for q in range(rows // step):
        r = q * step
        left = jnp.concatenate([part(r + 1 - u) for u in range(3)], axis=1)
        right = final[...].reshape(3 * channels, 3 * channels)
        sums = jnp.dot(left, right, preferred_element_type=F32)
        for n in range(step):
            piece = sums[n * width : (n + 1) * width]
            _, after = moved_columns(piece[:, :channels])
            before, _ = moved_columns(piece[:, 2 * channels :])
            done[q * step + n] = (piece[:, channels : 2 * channels] + after + before).astype(BF16)
        copy = pltpu.make_async_copy(done.at[pl.ds(q * step, step)], out.at[pl.ds(r, step)], sems.at[q])
        copy.start()
        copies.append(copy)
    for copy in copies:
        copy.wait()


def local(feature_map, cotangent, style, bank, selection):
    _, rows, width, channels = feature_map.shape
    fm = feature_map.reshape(rows, width, channels)
    cot = cotangent.reshape(rows, width, channels)
    banks, own_out, taps, _ = bank.shape
    groups = NX * NZ
    tile = lax.axis_index("tile")
    place = jnp.stack([tile // (NZ * NC), (tile // NC) % NZ, tile % NC]).astype(jnp.int32)
    dma = pltpu.SemaphoreType.DMA
    piece = (taps, own_out, channels)
    pair = (NZ,) + piece
    message_of = (taps + 1, own_out, channels)

    last, first = call(
        rows_body,
        (shape((width, channels), BF16),) * 2,
        [HBM],
        [dma((2, 1))],
        nbytes=10**6,
        vmem=60 << 20,
        name="rows",
    )(cot)
    count = lax.axis_size("tile")
    low = lax.ppermute(last, "tile", [(i, i + 1) for i in range(count - 1)])
    high = lax.ppermute(first, "tile", [(i + 1, i) for i in range(count - 1)])

    kernel, final = call(
        mix_body, (shape(piece, F32), shape(piece, BF16)), [SMEM, VMEM, VMEM], flops=5*10**9, nbytes=10**6, name="mix"
    )(selection, style, jnp.transpose(bank, (0, 2, 1, 3)))
    final_z = swap_z(final)
    final_c = swap_core(final)
    final_cz = swap_core(final_z)

    grad, ends = call(
        grad_body,
        (shape((taps, NC, groups, 16, channels), F32), shape((2, width, channels), BF16)),
        [SMEM, VMEM, VMEM],
        [
            pltpu.VMEM((NC, groups, 16, (rows + 2) * width), BF16),
            pltpu.VMEM((3, rows * width, channels), BF16),
        ],
        flops=2 * 9 * rows * width * channels * channels,
        nbytes=4 * rows * width * channels,
        vmem=24 << 20,
        name="grad",
    )(place, cot, fm)
    mine, theirs = call(
        edge_body,
        (shape((groups,) + piece, F32), shape((groups,) + piece, BF16)),
        [SMEM] + [VMEM] * 5,
        [pltpu.VMEM((NC, groups, 16, width), BF16)] * 2,
        flops=2 * 6 * width * channels * channels,
        nbytes=4 * 10**6,
        name="edge",
    )(place, grad, ends, low, high, final_z)

    own_x, one, two, three = call(
        split_x_body,
        (shape(pair, F32),) + (shape(pair, BF16),) * 3,
        [SMEM] + [VMEM] * 2,
        flops=10**6,
        nbytes=3 * 10**6,
        name="split_x",
    )(place, mine, swap_core(theirs))
    total, other = call(
        split_z_body,
        (shape(piece, F32), shape(message_of, BF16)),
        [SMEM] + [VMEM] * 9,
        flops=10**6,
        nbytes=10**6,
        name="split_z",
    )(place, style, own_x, shift_x(one, 1), shift_x(two, 2), shift_x(three, 3), final, final_z, final_c, final_cz)
    message, style_row = call(
        owner_body,
        (shape(message_of, BF16), shape((8, channels), F32)),
        [SMEM] + [VMEM] * 5,
        flops=10**6,
        nbytes=10**6,
        name="owner",
    )(selection, style, kernel, total, other, swap_z(other))

    kernels = call(
        kernels_body,
        shape((NZ * NC * taps + 1, own_out, channels), BF16),
        [VMEM] * 5,
        flops=10**9,
        nbytes=10**7,
        name="kernels",
    )(style_row, final, final_c, final_z, final_cz)
    finals = [kernels] + [shift_x(kernels, k) for k in range(1, NX)]

    over_l = [flip_l(message, k) for k in range(1, NL)]
    ahead = call(ahead_body, shape((NL,) + message_of, BF16), [VMEM] * NL, name="ahead")(message, *over_l)
    over_y = [shift_y(ahead, k) for k in range(1, NY)]

    input_grad, token = call(
        input_body,
        (shape((rows, width, channels), BF16), shape((8, 128), F32)),
        [SMEM] + [VMEM] * (NX + 4),
        [
            pltpu.VMEM((3, channels, 3 * channels), BF16),
            pltpu.VMEM((rows, width, channels), BF16),
            dma((8,)),
        ],
        flops=2 * 9 * rows * width * channels * channels,
        nbytes=4 * rows * width * channels,
        vmem=24 << 20,
        out=(HBM, VMEM),
        name="input",
    )(place, *finals, low, high, cot, ahead)

    style_part = call(style_body, shape((8, channels), F32), [VMEM] * (NX + 1), name="style")(*finals, token)
    bank_grad, style_grad = pl.pallas_call(
        banks_body,
        out_shape=(shape((banks,) + piece, F32), shape((1, channels), F32)),
        in_specs=[VMEM] * (NY + 2),
        out_specs=(HBM, VMEM),
        scratch_shapes=[pltpu.VMEM((banks,) + piece, F32), dma((taps,))],
        compiler_params=pltpu.CompilerParams(vmem_limit_bytes=16 << 20),
        cost_estimate=pl.CostEstimate(flops=10**7, bytes_accessed=3 * 10**6, transcendentals=0),
        name="banks",
    )(style_part, swap_core(style_part), ahead, *over_y)

    return (
        input_grad.reshape(feature_map.shape),
        style_grad,
        jnp.transpose(bank_grad, (0, 2, 1, 3)),
    )


def solution(mesh):
    in_specs = (
        P("img", "tile", None, None),
        P("img", "tile", None, None),
        P("img", None),
        P(None, "tile", None, None),
        P("img", None),
    )
    out_specs = (P("img", "tile", None, None), P("img", None), P(None, "tile", None, None))
    return jax.shard_map(local, mesh=mesh, in_specs=in_specs, out_specs=out_specs, check_vma=False)
```

```python
import functools

import jax
import jax.numpy as jnp
from jax import lax
from jax.experimental import pallas as pl
from jax.experimental.pallas import tpu as pltpu
from jax.sharding import PartitionSpec as P

epsilon = 1e-06
F32 = jnp.float32
BF16 = jnp.bfloat16
VMEM = pl.BlockSpec(memory_space=pltpu.VMEM)
SMEM = pl.BlockSpec(memory_space=pltpu.SMEM)
ANY = pl.BlockSpec(memory_space=pl.ANY)
HBM = pl.BlockSpec(memory_space=pltpu.HBM)

NX, NZ, NC = 4, 2, 2
NL, NY = 4, 4


def tile_perm(move):
    place = lambda x, z, c: (x * NZ + z) * NC + c
    return [
        (place(x, z, c), place(*move(x, z, c)))
        for x in range(NX)
        for z in range(NZ)
        for c in range(NC)
    ]


def img_perm(move):
    place = lambda l, y: l * NY + y
    return [(place(l, y), place(*move(l, y))) for l in range(NL) for y in range(NY)]


def swap_core(a):
    return lax.ppermute(a, "tile", tile_perm(lambda x, z, c: (x, z, 1 - c)))


def swap_z(a):
    return lax.ppermute(a, "tile", tile_perm(lambda x, z, c: (x, 1 - z, c)))


def shift_x(a, k):
    return lax.ppermute(a, "tile", tile_perm(lambda x, z, c: ((x + k) % NX, z, c)))


def flip_x(a, k):
    return lax.ppermute(a, "tile", tile_perm(lambda x, z, c: (x ^ k, z, c)))


def flip_l(a, k):
    return lax.ppermute(a, "img", img_perm(lambda l, y: (l ^ k, y)))


def shift_y(a, k):
    return lax.ppermute(a, "img", img_perm(lambda l, y: (l, (y + k) % NY)))


def two_first(shift, one, two, three):
    return [shift(two, 2), shift(one, 1), shift(three, 3)]


def call(body, outs, in_specs, scratch=(), flops=0, nbytes=0, vmem=16 << 20, out=VMEM, name=None):
    return pl.pallas_call(
        body,
        out_shape=outs,
        in_specs=in_specs,
        out_specs=out if isinstance(out, tuple) else jax.tree.map(lambda _: out, outs),
        scratch_shapes=list(scratch),
        compiler_params=pltpu.CompilerParams(vmem_limit_bytes=vmem),
        cost_estimate=pl.CostEstimate(flops=flops, bytes_accessed=nbytes, transcendentals=0),
        name=name,
    )


def shape(s, dtype):
    return jax.ShapeDtypeStruct(s, dtype)


def demod_of(kernel, style):
    total = None
    for t in range(kernel.shape[0]):
        modded = kernel[t] * style
        total = modded * modded if total is None else total + modded * modded
    return lax.rsqrt(jnp.sum(total, axis=1, keepdims=True) + epsilon)


def fetch(copies):
    for copy in copies:
        copy.start()
    for copy in copies:
        copy.wait()


def rows_body(cot, last, first, sems):
    rows, width = cot.shape[:2]
    parts = sems.shape[1]
    copies = []
    for n, (row, out) in enumerate(((rows - 1, last), (0, first))):
        for p in range(parts):
            here = pl.ds(p * (width // parts), width // parts)
            copies.append(pltpu.make_async_copy(cot.at[row, here], out.at[here], sems.at[n, p]))
    fetch(copies)


def mix_body(sel, style, bank, kernel, final):
    banks, taps = bank.shape[:2]
    top = sel.shape[1]
    weights = []
    for k in range(banks):
        w = F32(0)
        for j in range(top):
            w = w + jnp.where(sel[0, j] == k, F32((top - j) / (top * (top + 1) / 2)), F32(0))
        weights.append(w)
    for t in range(taps):
        mixed = None
        for k in range(banks):
            term = weights[k] * bank[k, t].astype(F32)
            mixed = term if mixed is None else mixed + term
        kernel[t] = mixed
    demod = demod_of(kernel, style[...])
    for t in range(taps):
        final[t] = (kernel[t] * style[...] * demod).astype(BF16)


def moved_columns(row):
    width = row.shape[0]
    column = lax.broadcasted_iota(jnp.int32, row.shape, 0)
    before = jnp.where(column == 0, F32(0), pltpu.roll(row, 1, 0))
    after = jnp.where(column == width - 1, F32(0), pltpu.roll(row, width - 1, 0))
    return before, after


def turned(row, core, out, at):
    width, channels = row.shape
    groups = channels // (16 * NC)
    flat = jnp.transpose(row)
    for g in range(groups):
        for c in range(NC):
            start = (g * NC + c) * 16
            out[c ^ core, g, :, at] = flat[start : start + 16]


def grad_body(place, cot, fm, grad, ends, cot_t, fm_v, step=4):
    rows, width, channels = cot.shape
    groups = channels // (16 * NC)
    core = place[2]
    parts = rows // step
    nothing = jnp.zeros((NC, groups, 16, width), BF16)
    cot_t[:, :, :, :width] = nothing
    cot_t[:, :, :, (rows + 1) * width :] = nothing

    def prepare(q):
        for r in range(q * step, (q + 1) * step):
            row = fm[r]
            before, after = moved_columns(row.astype(F32))
            here = pl.ds(r * width, width)
            fm_v[0, here] = before.astype(BF16)
            fm_v[1, here] = row
            fm_v[2, here] = after.astype(BF16)
            if r in (0, rows - 1):
                ends[int(r > 0)] = row
            turned(cot[r], core, cot_t, pl.ds((r + 1) * width, width))

    def add(q):
        for u in range(3):
            left = cot_t[:, :, :, pl.ds((q * step + 2 - u) * width, step * width)]
            left = left.reshape(channels, step * width)
            for v in range(3):
                right = fm_v[v, pl.ds(q * step * width, step * width)]
                out = jnp.dot(left, right, preferred_element_type=F32)
                out = out.reshape(NC, groups, 16, channels)
                grad[3 * u + v] = out if q == 0 else grad[3 * u + v] + out

    prepare(0)
    for q in range(parts):
        if q + 1 < parts:
            prepare(q + 1)
        add(q)


def edge_body(place, grad, ends, low, high, after, mine, theirs, turn_low, turn_high):
    del after
    taps, _, groups, _, channels = grad.shape
    width = low.shape[0]
    core = place[2]
    turned(low[...], core, turn_low, pl.ds(0, width))
    turned(high[...], core, turn_high, pl.ds(0, width))

    def put(t, value):
        for g in range(groups):
            mine[g, t] = value[0, g]
            theirs[g, t] = value[1, g].astype(BF16)

    for t in (3, 4, 5):
        put(t, grad[t])
    for turn, end, tap in ((turn_high, 1, 0), (turn_low, 0, 6)):
        whole = ends[end]
        before, after = moved_columns(whole.astype(F32))
        left = turn[...].reshape(channels, width)
        for v, right in enumerate((before.astype(BF16), whole, after.astype(BF16))):
            out = jnp.dot(left, right, preferred_element_type=F32)
            put(tap + v, grad[tap + v] + out.reshape(NC, groups, 16, channels))


def split_x_body(place, mine, got, own, one, two, three):
    x = place[0]
    for k, out in ((0, own), (1, one), (2, two), (3, three)):
        base = lax.rem(x + k, NX) * NZ
        for z in range(NZ):
            out[z] = (mine[base + z] + got[base + z].astype(F32)).astype(out.dtype)


def put_row(block, row):
    at = lax.broadcasted_iota(jnp.int32, block.shape, 0)
    out = jnp.zeros(block.shape, F32)
    for n in range(3):
        part = row.astype(BF16).astype(F32)
        out = jnp.where(at == n, part, out)
        row = row - part
    block[...] = out.astype(BF16)


def take_row(block):
    rows = block[...].astype(F32)
    return (rows[0:1] + rows[1:2]) + rows[2:3]


def split_z_body(place, style, mine, two, one, three, near, got, after, after_too, total, other):
    del after, after_too
    taps, outs, channels = total.shape
    z = place[1]
    share = jnp.zeros((outs, channels), F32)
    for k, source in enumerate((near, got)):
        at = z ^ k
        dot = jnp.zeros((outs, channels), F32)
        values = []
        for t in range(taps):
            value = mine[at, t] + one[at, t].astype(F32) + two[at, t].astype(F32) + three[at, t].astype(F32)
            if k == 0:
                total[t] = value
            else:
                other[t] = value.astype(BF16)
            dot = dot + value * source[t].astype(F32)
            values.append(value)
        dot = jnp.sum(dot, axis=1, keepdims=True)
        for t in range(taps):
            final = source[t].astype(F32)
            share = share + (values[t] - final * dot) * final
    put_row(other.at[taps], jnp.sum(share, axis=0, keepdims=True) / style[...])


def owner_body(sel, style, kernel, total, sent, got, message, style_row):
    taps, outs, channels = kernel.shape
    top = sel.shape[1]
    s = style[...]
    style_row[...] = jnp.broadcast_to(take_row(sent.at[taps]) + take_row(got.at[taps]), style_row.shape)
    demod = demod_of(kernel, s)
    dot = jnp.zeros((outs, channels), F32)
    for t in range(taps):
        grad = total[t] + got[t].astype(F32)
        dot = dot + grad * (kernel[t] * s)
    curvature = jnp.sum(dot, axis=1, keepdims=True)
    slope = demod * demod * demod * curvature
    for t in range(taps):
        grad = total[t] + got[t].astype(F32)
        modded_grad = demod * grad - slope * (kernel[t] * s)
        message[t] = (modded_grad * s).astype(BF16)
    bank = lax.broadcasted_iota(jnp.int32, (outs, channels), 0)
    rank = jnp.zeros((outs, channels), F32)
    for j in range(top):
        rank = rank + jnp.where(bank == sel[0, j], F32(top - j), F32(0))
    message[taps] = rank.astype(BF16)


def kernels_body(style_row, *refs):
    out = refs[-1]
    taps = refs[0].shape[0]
    for n, piece in enumerate(refs[:-1]):
        out[pl.ds(n * taps, taps)] = piece[...]
    put_row(out.at[(len(refs) - 1) * taps], style_row[0:1])


def style_body(*refs):
    out = refs[-1]
    zero, two, one, three = [take_row(ref.at[ref.shape[0] - 1]) for ref in refs[:NX]]
    out[...] = jnp.broadcast_to((zero + two) + (one + three), out.shape)


def ahead_body(*refs):
    out = refs[-1]
    for k, piece in enumerate(refs[:-1]):
        out[k] = piece[...]


def banks_body(*refs):
    out, both, sems = refs[-3:]
    banks, taps, outs, channels = out.shape
    pieces = []
    for ref in refs[:-3]:
        if len(ref.shape) == 3:
            pieces.append(ref)
        else:
            pieces.extend(ref.at[n] for n in range(ref.shape[0]))
    lane = lax.broadcasted_iota(jnp.int32, (outs, channels), 1)
    row = lax.broadcasted_iota(jnp.int32, (outs, channels), 0)
    ranks = jnp.zeros((outs, channels), F32)
    for n, piece in enumerate(pieces):
        ranks = jnp.where(lane // outs == n, piece[taps].astype(F32), ranks)
    left = jnp.concatenate(
        [jnp.where(lane % outs == row, ranks[k : k + 1], F32(0)) for k in range(banks)], axis=0
    ).astype(BF16)
    copies = []
    for t in range(taps):
        right = jnp.concatenate([piece[t] for piece in pieces], axis=0)
        total = jnp.dot(left, right, preferred_element_type=F32) / F32(6)
        both[:, t] = total.reshape(banks, outs, channels)
        copy = pltpu.make_async_copy(both.at[:, t], out.at[:, t], sems.at[t])
        copy.start()
        copies.append(copy)
    for copy in copies:
        copy.wait()


def input_body(place, *refs, step=2):
    finals = refs[:NX]
    low, high, cot, after, out, token, final, done, sems = refs[NX:]
    del after
    token[...] = jnp.zeros(token.shape, F32)
    rows, width, channels = cot.shape
    x, z, core = place[0], place[1], place[2]
    for k in range(NX):
        for n in range(NZ):
            for c in range(NC):
                at = (lax.rem(x + NX - (0, 2, 1, 3)[k], NX) * NZ + (z ^ n)) * NC + (core ^ c)
                here = pl.ds(pl.multiple_of(at * 16, 16), 16)
                for t in range(9):
                    u, v = t // 3, t % 3
                    final[u, here, v * channels : (v + 1) * channels] = finals[k][(n * NC + c) * 9 + t]

    def part(start):
        if start < 0:
            return jnp.concatenate([low[...], cot[0 : step - 1].reshape((step - 1) * width, channels)], axis=0)
        if start + step > rows:
            return jnp.concatenate([cot[start:rows].reshape((rows - start) * width, channels), high[...]], axis=0)
        return cot[start : start + step].reshape(step * width, channels)

    copies = []
    for q in range(rows // step):
        r = q * step
        left = jnp.concatenate([part(r + 1 - u) for u in range(3)], axis=1)
        right = final[...].reshape(3 * channels, 3 * channels)
        sums = jnp.dot(left, right, preferred_element_type=F32)
        for n in range(step):
            piece = sums[n * width : (n + 1) * width]
            _, after = moved_columns(piece[:, :channels])
            before, _ = moved_columns(piece[:, 2 * channels :])
            done[q * step + n] = (piece[:, channels : 2 * channels] + after + before).astype(BF16)
        copy = pltpu.make_async_copy(done.at[pl.ds(q * step, step)], out.at[pl.ds(r, step)], sems.at[q])
        copy.start()
        copies.append(copy)
    for copy in copies:
        copy.wait()


def local(feature_map, cotangent, style, bank, selection):
    _, rows, width, channels = feature_map.shape
    fm = feature_map.reshape(rows, width, channels)
    cot = cotangent.reshape(rows, width, channels)
    banks, own_out, taps, _ = bank.shape
    groups = NX * NZ
    tile = lax.axis_index("tile")
    place = jnp.stack([tile // (NZ * NC), (tile // NC) % NZ, tile % NC]).astype(jnp.int32)
    dma = pltpu.SemaphoreType.DMA
    piece = (taps, own_out, channels)
    pair = (NZ,) + piece
    message_of = (taps + 1, own_out, channels)

    last, first = call(
        rows_body,
        (shape((width, channels), BF16),) * 2,
        [HBM],
        [dma((2, 1))],
        nbytes=10**6,
        vmem=60 << 20,
        name="rows",
    )(cot)
    count = lax.axis_size("tile")
    low = lax.ppermute(last, "tile", [(i, i + 1) for i in range(count - 1)])
    high = lax.ppermute(first, "tile", [(i + 1, i) for i in range(count - 1)])

    kernel, final = call(
        mix_body, (shape(piece, F32), shape(piece, BF16)), [SMEM, VMEM, VMEM], flops=5*10**9, nbytes=10**6, name="mix"
    )(selection, style, jnp.transpose(bank, (0, 2, 1, 3)))
    final_z = swap_z(final)
    final_c = swap_core(final)
    final_cz = swap_core(final_z)

    grad, ends = call(
        grad_body,
        (shape((taps, NC, groups, 16, channels), F32), shape((2, width, channels), BF16)),
        [SMEM, VMEM, VMEM],
        [
            pltpu.VMEM((NC, groups, 16, (rows + 2) * width), BF16),
            pltpu.VMEM((3, rows * width, channels), BF16),
        ],
        flops=2 * 9 * rows * width * channels * channels,
        nbytes=4 * rows * width * channels,
        vmem=24 << 20,
        name="grad",
    )(place, cot, fm)
    mine, theirs = call(
        edge_body,
        (shape((groups,) + piece, F32), shape((groups,) + piece, BF16)),
        [SMEM] + [VMEM] * 5,
        [pltpu.VMEM((NC, groups, 16, width), BF16)] * 2,
        flops=2 * 6 * width * channels * channels,
        nbytes=4 * 10**6,
        name="edge",
    )(place, grad, ends, low, high, final_z)

    own_x, one, two, three = call(
        split_x_body,
        (shape(pair, F32),) + (shape(pair, BF16),) * 3,
        [SMEM] + [VMEM] * 2,
        flops=10**6,
        nbytes=3 * 10**6,
        name="split_x",
    )(place, mine, swap_core(theirs))
    x_got = two_first(shift_x, one, two, three)
    total, other = call(
        split_z_body,
        (shape(piece, F32), shape(message_of, BF16)),
        [SMEM] + [VMEM] * 9,
        flops=10**6,
        nbytes=10**6,
        name="split_z",
    )(place, style, own_x, *x_got, final, final_z, final_c, final_cz)
    message, style_row = call(
        owner_body,
        (shape(message_of, BF16), shape((8, channels), F32)),
        [SMEM] + [VMEM] * 5,
        flops=10**6,
        nbytes=10**6,
        name="owner",
    )(selection, style, kernel, total, other, swap_z(other))

    kernels = call(
        kernels_body,
        shape((NZ * NC * taps + 1, own_out, channels), BF16),
        [VMEM] * 5,
        flops=10**9,
        nbytes=10**7,
        name="kernels",
    )(style_row, final, final_c, final_z, final_cz)
    finals = [kernels] + two_first(shift_x, kernels, kernels, kernels)

    over_l = [flip_l(message, k) for k in range(1, NL)]
    ahead = call(ahead_body, shape((NL,) + message_of, BF16), [VMEM] * NL, name="ahead")(message, *over_l)
    over_y = two_first(shift_y, ahead, ahead, ahead)

    input_grad, token = call(
        input_body,
        (shape((rows, width, channels), BF16), shape((8, 128), F32)),
        [SMEM] + [VMEM] * (NX + 4),
        [
            pltpu.VMEM((3, channels, 3 * channels), BF16),
            pltpu.VMEM((rows, width, channels), BF16),
            dma((8,)),
        ],
        flops=2 * 9 * rows * width * channels * channels,
        nbytes=4 * rows * width * channels,
        vmem=24 << 20,
        out=(HBM, VMEM),
        name="input",
    )(place, *finals, low, high, cot, ahead)

    style_part = call(style_body, shape((8, channels), F32), [VMEM] * (NX + 1), name="style")(*finals, token)
    style_grad = (style_part + swap_core(style_part))[:1]
    bank_grad = pl.pallas_call(
        banks_body,
        out_shape=shape((banks,) + piece, F32),
        in_specs=[VMEM] * NY,
        out_specs=HBM,
        scratch_shapes=[pltpu.VMEM((banks,) + piece, F32), dma((taps,))],
        compiler_params=pltpu.CompilerParams(vmem_limit_bytes=16 << 20),
        cost_estimate=pl.CostEstimate(flops=10**7, bytes_accessed=3 * 10**6, transcendentals=0),
        name="banks",
    )(ahead, *over_y)

    return (
        input_grad.reshape(feature_map.shape),
        style_grad,
        jnp.transpose(bank_grad, (0, 2, 1, 3)),
    )


def solution(mesh):
    in_specs = (
        P("img", "tile", None, None),
        P("img", "tile", None, None),
        P("img", None),
        P(None, "tile", None, None),
        P("img", None),
    )
    out_specs = (P("img", "tile", None, None), P("img", None), P(None, "tile", None, None))
    return jax.shard_map(local, mesh=mesh, in_specs=in_specs, out_specs=out_specs, check_vma=False)
```

```python
import functools

import jax
import jax.numpy as jnp
from jax import lax
from jax.experimental import pallas as pl
from jax.experimental.pallas import tpu as pltpu
from jax.sharding import PartitionSpec as P

epsilon = 1e-06
F32 = jnp.float32
BF16 = jnp.bfloat16
VMEM = pl.BlockSpec(memory_space=pltpu.VMEM)
SMEM = pl.BlockSpec(memory_space=pltpu.SMEM)
ANY = pl.BlockSpec(memory_space=pl.ANY)
HBM = pl.BlockSpec(memory_space=pltpu.HBM)

NX, NZ, NC = 4, 2, 2
NL, NY = 4, 4


def tile_perm(move):
    place = lambda x, z, c: (x * NZ + z) * NC + c
    return [
        (place(x, z, c), place(*move(x, z, c)))
        for x in range(NX)
        for z in range(NZ)
        for c in range(NC)
    ]


def img_perm(move):
    place = lambda l, y: l * NY + y
    return [(place(l, y), place(*move(l, y))) for l in range(NL) for y in range(NY)]


def swap_core(a):
    return lax.ppermute(a, "tile", tile_perm(lambda x, z, c: (x, z, 1 - c)))


def swap_z(a):
    return lax.ppermute(a, "tile", tile_perm(lambda x, z, c: (x, 1 - z, c)))


def shift_x(a, k):
    return lax.ppermute(a, "tile", tile_perm(lambda x, z, c: ((x + k) % NX, z, c)))


def flip_x(a, k):
    return lax.ppermute(a, "tile", tile_perm(lambda x, z, c: (x ^ k, z, c)))


def flip_l(a, k):
    return lax.ppermute(a, "img", img_perm(lambda l, y: (l ^ k, y)))


def shift_y(a, k):
    return lax.ppermute(a, "img", img_perm(lambda l, y: (l, (y + k) % NY)))


def two_first(shift, one, two, three):
    return [shift(two, 2), shift(one, 1), shift(three, 3)]


def call(body, outs, in_specs, scratch=(), flops=0, nbytes=0, vmem=16 << 20, out=VMEM, name=None):
    return pl.pallas_call(
        body,
        out_shape=outs,
        in_specs=in_specs,
        out_specs=out if isinstance(out, tuple) else jax.tree.map(lambda _: out, outs),
        scratch_shapes=list(scratch),
        compiler_params=pltpu.CompilerParams(vmem_limit_bytes=vmem),
        cost_estimate=pl.CostEstimate(flops=flops, bytes_accessed=nbytes, transcendentals=0),
        name=name,
    )


def shape(s, dtype):
    return jax.ShapeDtypeStruct(s, dtype)


def demod_of(kernel, style):
    total = None
    for t in range(kernel.shape[0]):
        modded = kernel[t] * style
        total = modded * modded if total is None else total + modded * modded
    return lax.rsqrt(jnp.sum(total, axis=1, keepdims=True) + epsilon)


def fetch(copies):
    for copy in copies:
        copy.start()
    for copy in copies:
        copy.wait()


def rows_body(cot, last, first, sems):
    rows, width = cot.shape[:2]
    parts = sems.shape[1]
    copies = []
    for n, (row, out) in enumerate(((rows - 1, last), (0, first))):
        for p in range(parts):
            here = pl.ds(p * (width // parts), width // parts)
            copies.append(pltpu.make_async_copy(cot.at[row, here], out.at[here], sems.at[n, p]))
    fetch(copies)


def mix_body(sel, style, bank, kernel, final):
    banks, taps = bank.shape[:2]
    top = sel.shape[1]
    weights = []
    for k in range(banks):
        w = F32(0)
        for j in range(top):
            w = w + jnp.where(sel[0, j] == k, F32((top - j) / (top * (top + 1) / 2)), F32(0))
        weights.append(w)
    for t in range(taps):
        mixed = None
        for k in range(banks):
            term = weights[k] * bank[k, t].astype(F32)
            mixed = term if mixed is None else mixed + term
        kernel[t] = mixed
    demod = demod_of(kernel, style[...])
    for t in range(taps):
        final[t] = (kernel[t] * style[...] * demod).astype(BF16)


def moved_columns(row):
    width = row.shape[0]
    column = lax.broadcasted_iota(jnp.int32, row.shape, 0)
    before = jnp.where(column == 0, F32(0), pltpu.roll(row, 1, 0))
    after = jnp.where(column == width - 1, F32(0), pltpu.roll(row, width - 1, 0))
    return before, after


def turned(row, core, out, at):
    width, channels = row.shape
    groups = channels // (16 * NC)
    flat = jnp.transpose(row)
    for g in range(groups):
        for c in range(NC):
            start = (g * NC + c) * 16
            out[c ^ core, g, :, at] = flat[start : start + 16]


def grad_body(place, cot, fm, grad, ends, cot_t, fm_v, step=4):
    rows, width, channels = cot.shape
    groups = channels // (16 * NC)
    core = place[2]
    parts = rows // step
    nothing = jnp.zeros((NC, groups, 16, width), BF16)
    cot_t[:, :, :, :width] = nothing
    cot_t[:, :, :, (rows + 1) * width :] = nothing

    def prepare(q):
        for r in range(q * step, (q + 1) * step):
            row = fm[r]
            before, after = moved_columns(row.astype(F32))
            here = pl.ds(r * width, width)
            fm_v[0, here] = before.astype(BF16)
            fm_v[1, here] = row
            fm_v[2, here] = after.astype(BF16)
            if r in (0, rows - 1):
                ends[int(r > 0)] = row
            turned(cot[r], core, cot_t, pl.ds((r + 1) * width, width))

    def add(q):
        for u in range(3):
            left = cot_t[:, :, :, pl.ds((q * step + 2 - u) * width, step * width)]
            left = left.reshape(channels, step * width)
            for v in range(3):
                right = fm_v[v, pl.ds(q * step * width, step * width)]
                out = jnp.dot(left, right, preferred_element_type=F32)
                out = out.reshape(NC, groups, 16, channels)
                grad[3 * u + v] = out if q == 0 else grad[3 * u + v] + out

    prepare(0)
    for q in range(parts):
        if q + 1 < parts:
            prepare(q + 1)
        add(q)


def edge_body(place, grad, ends, low, high, after, mine, theirs, turn_low, turn_high):
    del after
    taps, _, groups, _, channels = grad.shape
    width = low.shape[0]
    core = place[2]
    turned(low[...], core, turn_low, pl.ds(0, width))
    turned(high[...], core, turn_high, pl.ds(0, width))

    def put(t, value):
        for g in range(groups):
            mine[g, t] = value[0, g]
            theirs[g, t] = value[1, g].astype(BF16)

    for t in (3, 4, 5):
        put(t, grad[t])
    for turn, end, tap in ((turn_high, 1, 0), (turn_low, 0, 6)):
        whole = ends[end]
        before, after = moved_columns(whole.astype(F32))
        left = turn[...].reshape(channels, width)
        for v, right in enumerate((before.astype(BF16), whole, after.astype(BF16))):
            out = jnp.dot(left, right, preferred_element_type=F32)
            put(tap + v, grad[tap + v] + out.reshape(NC, groups, 16, channels))


def split_x_body(place, mine, got, own, one, two, three):
    x = place[0]
    for k, out in ((0, own), (1, one), (2, two), (3, three)):
        base = lax.rem(x + k, NX) * NZ
        for z in range(NZ):
            out[z] = (mine[base + z] + got[base + z].astype(F32)).astype(out.dtype)


def put_row(block, row):
    at = lax.broadcasted_iota(jnp.int32, block.shape, 0)
    out = jnp.zeros(block.shape, F32)
    for n in range(3):
        part = row.astype(BF16).astype(F32)
        out = jnp.where(at == n, part, out)
        row = row - part
    block[...] = out.astype(BF16)


def take_row(block):
    rows = block[...].astype(F32)
    return (rows[0:1] + rows[1:2]) + rows[2:3]


def split_z_body(place, style, mine, two, one, three, near, got, after, after_too, total, other):
    del after, after_too
    taps, outs, channels = total.shape
    z = place[1]
    share = jnp.zeros((outs, channels), F32)
    for k, source in enumerate((near, got)):
        at = z ^ k
        dot = jnp.zeros((outs, channels), F32)
        values = []
        for t in range(taps):
            value = mine[at, t] + one[at, t].astype(F32) + two[at, t].astype(F32) + three[at, t].astype(F32)
            if k == 0:
                total[t] = value
            else:
                other[t] = value.astype(BF16)
            dot = dot + value * source[t].astype(F32)
            values.append(value)
        dot = jnp.sum(dot, axis=1, keepdims=True)
        for t in range(taps):
            final = source[t].astype(F32)
            share = share + (values[t] - final * dot) * final
    put_row(other.at[taps], jnp.sum(share, axis=0, keepdims=True) / style[...])


def owner_body(sel, style, kernel, total, sent, got, message, style_row):
    taps, outs, channels = kernel.shape
    top = sel.shape[1]
    s = style[...]
    style_row[...] = jnp.broadcast_to(take_row(sent.at[taps]) + take_row(got.at[taps]), style_row.shape)
    demod = demod_of(kernel, s)
    dot = jnp.zeros((outs, channels), F32)
    for t in range(taps):
        grad = total[t] + got[t].astype(F32)
        dot = dot + grad * (kernel[t] * s)
    curvature = jnp.sum(dot, axis=1, keepdims=True)
    slope = demod * demod * demod * curvature
    for t in range(taps):
        grad = total[t] + got[t].astype(F32)
        modded_grad = demod * grad - slope * (kernel[t] * s)
        message[t] = (modded_grad * s).astype(BF16)
    bank = lax.broadcasted_iota(jnp.int32, (outs, channels), 0)
    rank = jnp.zeros((outs, channels), F32)
    for j in range(top):
        rank = rank + jnp.where(bank == sel[0, j], F32(top - j), F32(0))
    message[taps] = rank.astype(BF16)


def kernels_body(style_row, *refs):
    out = refs[-1]
    taps = refs[0].shape[0]
    for n, piece in enumerate(refs[:-1]):
        out[pl.ds(n * taps, taps)] = piece[...]
    put_row(out.at[(len(refs) - 1) * taps], style_row[0:1])


def style_body(*refs):
    out = refs[-1]
    zero, two, one, three = [take_row(ref.at[ref.shape[0] - 1]) for ref in refs[:NX]]
    out[...] = jnp.broadcast_to((zero + two) + (one + three), out.shape)


def add_body(one, two, token, out):
    del token
    out[...] = one[0:1] + two[0:1]


def ahead_body(*refs):
    out = refs[-1]
    for k, piece in enumerate(refs[:-1]):
        out[k] = piece[...]


def banks_body(*refs):
    out, token, both, sems = refs[-4:]
    banks, taps, outs, channels = out.shape
    token[...] = jnp.zeros(token.shape, F32)
    pieces = []
    for ref in refs[:-4]:
        if len(ref.shape) == 3:
            pieces.append(ref)
        else:
            pieces.extend(ref.at[n] for n in range(ref.shape[0]))
    lane = lax.broadcasted_iota(jnp.int32, (outs, channels), 1)
    row = lax.broadcasted_iota(jnp.int32, (outs, channels), 0)
    ranks = jnp.zeros((outs, channels), F32)
    for n, piece in enumerate(pieces):
        ranks = jnp.where(lane // outs == n, piece[taps].astype(F32), ranks)
    left = jnp.concatenate(
        [jnp.where(lane % outs == row, ranks[k : k + 1], F32(0)) for k in range(banks)], axis=0
    ).astype(BF16)
    copies = []
    for t in range(taps):
        right = jnp.concatenate([piece[t] for piece in pieces], axis=0)
        total = jnp.dot(left, right, preferred_element_type=F32) / F32(6)
        both[:, t] = total.reshape(banks, outs, channels)
        copy = pltpu.make_async_copy(both.at[:, t], out.at[:, t], sems.at[t])
        copy.start()
        copies.append(copy)
    for copy in copies:
        copy.wait()


def input_body(place, *refs, step=2):
    finals = refs[:NX]
    low, high, cot, after, out, token, final, done, sems = refs[NX:]
    del after
    token[...] = jnp.zeros(token.shape, F32)
    rows, width, channels = cot.shape
    x, z, core = place[0], place[1], place[2]
    for k in range(NX):
        for n in range(NZ):
            for c in range(NC):
                at = (lax.rem(x + NX - (0, 2, 1, 3)[k], NX) * NZ + (z ^ n)) * NC + (core ^ c)
                here = pl.ds(pl.multiple_of(at * 16, 16), 16)
                for t in range(9):
                    u, v = t // 3, t % 3
                    final[u, here, v * channels : (v + 1) * channels] = finals[k][(n * NC + c) * 9 + t]

    def part(start):
        if start < 0:
            return jnp.concatenate([low[...], cot[0 : step - 1].reshape((step - 1) * width, channels)], axis=0)
        if start + step > rows:
            return jnp.concatenate([cot[start:rows].reshape((rows - start) * width, channels), high[...]], axis=0)
        return cot[start : start + step].reshape(step * width, channels)

    copies = []
    for q in range(rows // step):
        r = q * step
        left = jnp.concatenate([part(r + 1 - u) for u in range(3)], axis=1)
        right = final[...].reshape(3 * channels, 3 * channels)
        sums = jnp.dot(left, right, preferred_element_type=F32)
        for n in range(step):
            piece = sums[n * width : (n + 1) * width]
            _, after = moved_columns(piece[:, :channels])
            before, _ = moved_columns(piece[:, 2 * channels :])
            done[q * step + n] = (piece[:, channels : 2 * channels] + after + before).astype(BF16)
        copy = pltpu.make_async_copy(done.at[pl.ds(q * step, step)], out.at[pl.ds(r, step)], sems.at[q])
        copy.start()
        copies.append(copy)
    for copy in copies:
        copy.wait()


def local(feature_map, cotangent, style, bank, selection):
    _, rows, width, channels = feature_map.shape
    fm = feature_map.reshape(rows, width, channels)
    cot = cotangent.reshape(rows, width, channels)
    banks, own_out, taps, _ = bank.shape
    groups = NX * NZ
    tile = lax.axis_index("tile")
    place = jnp.stack([tile // (NZ * NC), (tile // NC) % NZ, tile % NC]).astype(jnp.int32)
    dma = pltpu.SemaphoreType.DMA
    piece = (taps, own_out, channels)
    pair = (NZ,) + piece
    message_of = (taps + 1, own_out, channels)

    last, first = call(
        rows_body,
        (shape((width, channels), BF16),) * 2,
        [HBM],
        [dma((2, 1))],
        nbytes=10**6,
        vmem=60 << 20,
        name="rows",
    )(cot)
    count = lax.axis_size("tile")
    low = lax.ppermute(last, "tile", [(i, i + 1) for i in range(count - 1)])
    high = lax.ppermute(first, "tile", [(i + 1, i) for i in range(count - 1)])

    kernel, final = call(
        mix_body, (shape(piece, F32), shape(piece, BF16)), [SMEM, VMEM, VMEM], flops=5*10**9, nbytes=10**6, name="mix"
    )(selection, style, jnp.transpose(bank, (0, 2, 1, 3)))
    final_z = swap_z(final)
    final_c = swap_core(final)
    final_cz = swap_core(final_z)

    grad, ends = call(
        grad_body,
        (shape((taps, NC, groups, 16, channels), F32), shape((2, width, channels), BF16)),
        [SMEM, VMEM, VMEM],
        [
            pltpu.VMEM((NC, groups, 16, (rows + 2) * width), BF16),
            pltpu.VMEM((3, rows * width, channels), BF16),
        ],
        flops=2 * 9 * rows * width * channels * channels,
        nbytes=4 * rows * width * channels,
        vmem=24 << 20,
        name="grad",
    )(place, cot, fm)
    mine, theirs = call(
        edge_body,
        (shape((groups,) + piece, F32), shape((groups,) + piece, BF16)),
        [SMEM] + [VMEM] * 5,
        [pltpu.VMEM((NC, groups, 16, width), BF16)] * 2,
        flops=2 * 6 * width * channels * channels,
        nbytes=4 * 10**6,
        name="edge",
    )(place, grad, ends, low, high, final_z)

    own_x, one, two, three = call(
        split_x_body,
        (shape(pair, F32),) + (shape(pair, BF16),) * 3,
        [SMEM] + [VMEM] * 2,
        flops=10**6,
        nbytes=3 * 10**6,
        name="split_x",
    )(place, mine, swap_core(theirs))
    x_got = two_first(shift_x, one, two, three)
    total, other = call(
        split_z_body,
        (shape(piece, F32), shape(message_of, BF16)),
        [SMEM] + [VMEM] * 9,
        flops=10**6,
        nbytes=10**6,
        name="split_z",
    )(place, style, own_x, *x_got, final, final_z, final_c, final_cz)
    message, style_row = call(
        owner_body,
        (shape(message_of, BF16), shape((8, channels), F32)),
        [SMEM] + [VMEM] * 5,
        flops=10**6,
        nbytes=10**6,
        name="owner",
    )(selection, style, kernel, total, other, swap_z(other))

    kernels = call(
        kernels_body,
        shape((NZ * NC * taps + 1, own_out, channels), BF16),
        [VMEM] * 5,
        flops=10**9,
        nbytes=10**7,
        name="kernels",
    )(style_row, final, final_c, final_z, final_cz)
    finals = [kernels] + two_first(shift_x, kernels, kernels, kernels)

    over_l = [flip_l(message, k) for k in range(1, NL)]
    ahead = call(ahead_body, shape((NL,) + message_of, BF16), [VMEM] * NL, name="ahead")(message, *over_l)
    over_y = two_first(shift_y, ahead, ahead, ahead)

    input_grad, token = call(
        input_body,
        (shape((rows, width, channels), BF16), shape((8, 128), F32)),
        [SMEM] + [VMEM] * (NX + 4),
        [
            pltpu.VMEM((3, channels, 3 * channels), BF16),
            pltpu.VMEM((rows, width, channels), BF16),
            dma((8,)),
        ],
        flops=2 * 9 * rows * width * channels * channels,
        nbytes=4 * rows * width * channels,
        vmem=24 << 20,
        out=(HBM, VMEM),
        name="input",
    )(place, *finals, low, high, cot, ahead)

    style_part = call(style_body, shape((8, channels), F32), [VMEM] * (NX + 1), name="style")(*finals, token)
    bank_grad, token = pl.pallas_call(
        banks_body,
        out_shape=(shape((banks,) + piece, F32), shape((8, 128), F32)),
        in_specs=[VMEM] * NY,
        out_specs=(HBM, VMEM),
        scratch_shapes=[pltpu.VMEM((banks,) + piece, F32), dma((taps,))],
        compiler_params=pltpu.CompilerParams(vmem_limit_bytes=16 << 20),
        cost_estimate=pl.CostEstimate(flops=10**7, bytes_accessed=3 * 10**6, transcendentals=0),
        name="banks",
    )(ahead, *over_y)
    style_grad = call(add_body, shape((1, channels), F32), [VMEM] * 3, name="add")(
        style_part, swap_core(style_part), token
    )

    return (
        input_grad.reshape(feature_map.shape),
        style_grad,
        jnp.transpose(bank_grad, (0, 2, 1, 3)),
    )


def solution(mesh):
    in_specs = (
        P("img", "tile", None, None),
        P("img", "tile", None, None),
        P("img", None),
        P(None, "tile", None, None),
        P("img", None),
    )
    out_specs = (P("img", "tile", None, None), P("img", None), P(None, "tile", None, None))
    return jax.shard_map(local, mesh=mesh, in_specs=in_specs, out_specs=out_specs, check_vma=False)
```

```python
import functools

import jax
import jax.numpy as jnp
from jax import lax
from jax.experimental import pallas as pl
from jax.experimental.pallas import tpu as pltpu
from jax.sharding import PartitionSpec as P

epsilon = 1e-06
F32 = jnp.float32
BF16 = jnp.bfloat16
VMEM = pl.BlockSpec(memory_space=pltpu.VMEM)
SMEM = pl.BlockSpec(memory_space=pltpu.SMEM)
ANY = pl.BlockSpec(memory_space=pl.ANY)
HBM = pl.BlockSpec(memory_space=pltpu.HBM)

NX, NZ, NC = 4, 2, 2
NL, NY = 4, 4


def tile_perm(move):
    place = lambda x, z, c: (x * NZ + z) * NC + c
    return [
        (place(x, z, c), place(*move(x, z, c)))
        for x in range(NX)
        for z in range(NZ)
        for c in range(NC)
    ]


def img_perm(move):
    place = lambda l, y: l * NY + y
    return [(place(l, y), place(*move(l, y))) for l in range(NL) for y in range(NY)]


def swap_core(a):
    return lax.ppermute(a, "tile", tile_perm(lambda x, z, c: (x, z, 1 - c)))


def swap_z(a):
    return lax.ppermute(a, "tile", tile_perm(lambda x, z, c: (x, 1 - z, c)))


def shift_x(a, k):
    return lax.ppermute(a, "tile", tile_perm(lambda x, z, c: ((x + k) % NX, z, c)))


def flip_x(a, k):
    return lax.ppermute(a, "tile", tile_perm(lambda x, z, c: (x ^ k, z, c)))


def flip_l(a, k):
    return lax.ppermute(a, "img", img_perm(lambda l, y: (l ^ k, y)))


def shift_y(a, k):
    return lax.ppermute(a, "img", img_perm(lambda l, y: (l, (y + k) % NY)))


def two_first(shift, one, two, three):
    return [shift(two, 2), shift(one, 1), shift(three, 3)]


def call(body, outs, in_specs, scratch=(), flops=0, nbytes=0, vmem=16 << 20, out=VMEM, name=None):
    return pl.pallas_call(
        body,
        out_shape=outs,
        in_specs=in_specs,
        out_specs=out if isinstance(out, tuple) else jax.tree.map(lambda _: out, outs),
        scratch_shapes=list(scratch),
        compiler_params=pltpu.CompilerParams(vmem_limit_bytes=vmem),
        cost_estimate=pl.CostEstimate(flops=flops, bytes_accessed=nbytes, transcendentals=0),
        name=name,
    )


def shape(s, dtype):
    return jax.ShapeDtypeStruct(s, dtype)


def demod_of(kernel, style):
    total = None
    for t in range(kernel.shape[0]):
        modded = kernel[t] * style
        total = modded * modded if total is None else total + modded * modded
    return lax.rsqrt(jnp.sum(total, axis=1, keepdims=True) + epsilon)


def fetch(copies):
    for copy in copies:
        copy.start()
    for copy in copies:
        copy.wait()


def rows_body(cot, last, first, sems):
    rows, width = cot.shape[:2]
    parts = sems.shape[1]
    copies = []
    for n, (row, out) in enumerate(((rows - 1, last), (0, first))):
        for p in range(parts):
            here = pl.ds(p * (width // parts), width // parts)
            copies.append(pltpu.make_async_copy(cot.at[row, here], out.at[here], sems.at[n, p]))
    fetch(copies)


def mix_body(sel, style, bank, kernel, final):
    banks, taps = bank.shape[:2]
    top = sel.shape[1]
    weights = []
    for k in range(banks):
        w = F32(0)
        for j in range(top):
            w = w + jnp.where(sel[0, j] == k, F32((top - j) / (top * (top + 1) / 2)), F32(0))
        weights.append(w)
    for t in range(taps):
        mixed = None
        for k in range(banks):
            term = weights[k] * bank[k, t].astype(F32)
            mixed = term if mixed is None else mixed + term
        kernel[t] = mixed
    demod = demod_of(kernel, style[...])
    for t in range(taps):
        final[t] = (kernel[t] * style[...] * demod).astype(BF16)


def moved_columns(row):
    width = row.shape[0]
    column = lax.broadcasted_iota(jnp.int32, row.shape, 0)
    before = jnp.where(column == 0, F32(0), pltpu.roll(row, 1, 0))
    after = jnp.where(column == width - 1, F32(0), pltpu.roll(row, width - 1, 0))
    return before, after


def turned(row, core, out, at):
    width, channels = row.shape
    groups = channels // (16 * NC)
    flat = jnp.transpose(row)
    for g in range(groups):
        for c in range(NC):
            start = (g * NC + c) * 16
            out[c ^ core, g, :, at] = flat[start : start + 16]


def grad_body(place, cot, fm, grad, ends, cot_t, fm_v, step=4):
    rows, width, channels = cot.shape
    groups = channels // (16 * NC)
    core = place[2]
    parts = rows // step
    nothing = jnp.zeros((NC, groups, 16, width), BF16)
    cot_t[:, :, :, :width] = nothing
    cot_t[:, :, :, (rows + 1) * width :] = nothing

    def prepare(q):
        for r in range(q * step, (q + 1) * step):
            row = fm[r]
            before, after = moved_columns(row.astype(F32))
            here = pl.ds(r * width, width)
            fm_v[0, here] = before.astype(BF16)
            fm_v[1, here] = row
            fm_v[2, here] = after.astype(BF16)
            if r in (0, rows - 1):
                ends[int(r > 0)] = row
            turned(cot[r], core, cot_t, pl.ds((r + 1) * width, width))

    def add(q):
        for u in range(3):
            left = cot_t[:, :, :, pl.ds((q * step + 2 - u) * width, step * width)]
            left = left.reshape(channels, step * width)
            for v in range(3):
                right = fm_v[v, pl.ds(q * step * width, step * width)]
                out = jnp.dot(left, right, preferred_element_type=F32)
                out = out.reshape(NC, groups, 16, channels)
                grad[3 * u + v] = out if q == 0 else grad[3 * u + v] + out

    prepare(0)
    for q in range(parts):
        if q + 1 < parts:
            prepare(q + 1)
        add(q)


def edge_body(place, grad, ends, low, high, after, mine, theirs, turn_low, turn_high):
    del after
    taps, _, groups, _, channels = grad.shape
    width = low.shape[0]
    core = place[2]
    turned(low[...], core, turn_low, pl.ds(0, width))
    turned(high[...], core, turn_high, pl.ds(0, width))

    def put(t, value):
        for g in range(groups):
            mine[g, t] = value[0, g]
            theirs[g, t] = value[1, g].astype(BF16)

    for t in (3, 4, 5):
        put(t, grad[t])
    for turn, end, tap in ((turn_high, 1, 0), (turn_low, 0, 6)):
        whole = ends[end]
        before, after = moved_columns(whole.astype(F32))
        left = turn[...].reshape(channels, width)
        for v, right in enumerate((before.astype(BF16), whole, after.astype(BF16))):
            out = jnp.dot(left, right, preferred_element_type=F32)
            put(tap + v, grad[tap + v] + out.reshape(NC, groups, 16, channels))


def split_x_body(place, mine, got, own, one, two, three):
    x = place[0]
    for k, out in ((0, own), (1, one), (2, two), (3, three)):
        base = lax.rem(x + k, NX) * NZ
        for z in range(NZ):
            out[z] = (mine[base + z] + got[base + z].astype(F32)).astype(out.dtype)


def put_row(block, row):
    at = lax.broadcasted_iota(jnp.int32, block.shape, 0)
    out = jnp.zeros(block.shape, F32)
    for n in range(3):
        part = row.astype(BF16).astype(F32)
        out = jnp.where(at == n, part, out)
        row = row - part
    block[...] = out.astype(BF16)


def take_row(block):
    rows = block[...].astype(F32)
    return (rows[0:1] + rows[1:2]) + rows[2:3]


def split_z_body(place, style, mine, two, one, three, near, got, after, after_too, total, other):
    del after, after_too
    taps, outs, channels = total.shape
    z = place[1]
    share = jnp.zeros((outs, channels), F32)
    for k, source in enumerate((near, got)):
        at = z ^ k
        dot = jnp.zeros((outs, channels), F32)
        values = []
        for t in range(taps):
            value = mine[at, t] + one[at, t].astype(F32) + two[at, t].astype(F32) + three[at, t].astype(F32)
            if k == 0:
                total[t] = value
            else:
                other[t] = value.astype(BF16)
            dot = dot + value * source[t].astype(F32)
            values.append(value)
        dot = jnp.sum(dot, axis=1, keepdims=True)
        for t in range(taps):
            final = source[t].astype(F32)
            share = share + (values[t] - final * dot) * final
    put_row(other.at[taps], jnp.sum(share, axis=0, keepdims=True) / style[...])


def owner_body(sel, style, kernel, total, sent, got, message, style_row):
    taps, outs, channels = kernel.shape
    top = sel.shape[1]
    s = style[...]
    style_row[...] = jnp.broadcast_to(take_row(sent.at[taps]) + take_row(got.at[taps]), style_row.shape)
    demod = demod_of(kernel, s)
    dot = jnp.zeros((outs, channels), F32)
    for t in range(taps):
        grad = total[t] + got[t].astype(F32)
        dot = dot + grad * (kernel[t] * s)
    curvature = jnp.sum(dot, axis=1, keepdims=True)
    slope = demod * demod * demod * curvature
    for t in range(taps):
        grad = total[t] + got[t].astype(F32)
        modded_grad = demod * grad - slope * (kernel[t] * s)
        message[t] = (modded_grad * s).astype(BF16)
    bank = lax.broadcasted_iota(jnp.int32, (outs, channels), 0)
    rank = jnp.zeros((outs, channels), F32)
    for j in range(top):
        rank = rank + jnp.where(bank == sel[0, j], F32(top - j), F32(0))
    message[taps] = rank.astype(BF16)


def kernels_body(style_row, *refs):
    out = refs[-1]
    taps = refs[0].shape[0]
    for n, piece in enumerate(refs[:-1]):
        out[pl.ds(n * taps, taps)] = piece[...]
    put_row(out.at[(len(refs) - 1) * taps], style_row[0:1])


def style_body(*refs):
    out = refs[-1]
    zero, two, one, three = [take_row(ref.at[ref.shape[0] - 1]) for ref in refs[:NX]]
    out[...] = jnp.broadcast_to((zero + two) + (one + three), out.shape)


def add_body(one, two, token, out):
    del token
    out[...] = one[0:1] + two[0:1]


def ahead_body(*refs):
    out = refs[-1]
    for k, piece in enumerate(refs[:-1]):
        out[k] = piece[...]


def banks_body(*refs):
    out, token, both, sems = refs[-4:]
    banks, taps, outs, channels = out.shape
    token[...] = jnp.zeros(token.shape, F32)
    pieces = []
    for ref in refs[:-4]:
        if len(ref.shape) == 3:
            pieces.append(ref)
        else:
            pieces.extend(ref.at[n] for n in range(ref.shape[0]))
    lane = lax.broadcasted_iota(jnp.int32, (outs, channels), 1)
    row = lax.broadcasted_iota(jnp.int32, (outs, channels), 0)
    ranks = jnp.zeros((outs, channels), F32)
    for n, piece in enumerate(pieces):
        ranks = jnp.where(lane // outs == n, piece[taps].astype(F32), ranks)
    left = jnp.concatenate(
        [jnp.where(lane % outs == row, ranks[k : k + 1], F32(0)) for k in range(banks)], axis=0
    ).astype(BF16)
    copies = []
    for t in range(taps):
        right = jnp.concatenate([piece[t] for piece in pieces], axis=0)
        total = jnp.dot(left, right, preferred_element_type=F32) / F32(6)
        both[:, t] = total.reshape(banks, outs, channels)
        copy = pltpu.make_async_copy(both.at[:, t], out.at[:, t], sems.at[t])
        copy.start()
        copies.append(copy)
    for copy in copies:
        copy.wait()


def input_body(place, *refs, step=2):
    finals = refs[:NX]
    low, high, cot, after, out, token, final, done, sems = refs[NX:]
    del after
    token[...] = jnp.zeros(token.shape, F32)
    rows, width, channels = cot.shape
    x, z, core = place[0], place[1], place[2]
    for k in range(NX):
        for n in range(NZ):
            for c in range(NC):
                at = (lax.rem(x + NX - (0, 2, 1, 3)[k], NX) * NZ + (z ^ n)) * NC + (core ^ c)
                here = pl.ds(pl.multiple_of(at * 16, 16), 16)
                for t in range(9):
                    u, v = t // 3, t % 3
                    final[u, here, v * channels : (v + 1) * channels] = finals[k][(n * NC + c) * 9 + t]

    def part(start):
        if start < 0:
            return jnp.concatenate([low[...], cot[0 : step - 1].reshape((step - 1) * width, channels)], axis=0)
        if start + step > rows:
            return jnp.concatenate([cot[start:rows].reshape((rows - start) * width, channels), high[...]], axis=0)
        return cot[start : start + step].reshape(step * width, channels)

    copies = []
    for q in range(rows // step):
        r = q * step
        left = jnp.concatenate([part(r + 1 - u) for u in range(3)], axis=1)
        right = final[...].reshape(3 * channels, 3 * channels)
        sums = jnp.dot(left, right, preferred_element_type=F32)
        for n in range(step):
            piece = sums[n * width : (n + 1) * width]
            _, after = moved_columns(piece[:, :channels])
            before, _ = moved_columns(piece[:, 2 * channels :])
            done[q * step + n] = (piece[:, channels : 2 * channels] + after + before).astype(BF16)
        copy = pltpu.make_async_copy(done.at[pl.ds(q * step, step)], out.at[pl.ds(r, step)], sems.at[q])
        copy.start()
        copies.append(copy)
    for copy in copies:
        copy.wait()


def local(feature_map, cotangent, style, bank, selection):
    _, rows, width, channels = feature_map.shape
    fm = feature_map.reshape(rows, width, channels)
    cot = cotangent.reshape(rows, width, channels)
    banks, own_out, taps, _ = bank.shape
    groups = NX * NZ
    tile = lax.axis_index("tile")
    place = jnp.stack([tile // (NZ * NC), (tile // NC) % NZ, tile % NC]).astype(jnp.int32)
    dma = pltpu.SemaphoreType.DMA
    piece = (taps, own_out, channels)
    pair = (NZ,) + piece
    message_of = (taps + 1, own_out, channels)

    last, first = call(
        rows_body,
        (shape((width, channels), BF16),) * 2,
        [HBM],
        [dma((2, 1))],
        nbytes=10**6,
        vmem=60 << 20,
        name="rows",
    )(cot)
    count = lax.axis_size("tile")
    low = lax.ppermute(last, "tile", [(i, i + 1) for i in range(count - 1)])
    high = lax.ppermute(first, "tile", [(i + 1, i) for i in range(count - 1)])

    kernel, final = call(
        mix_body, (shape(piece, F32), shape(piece, BF16)), [SMEM, VMEM, VMEM], flops=5*10**9, nbytes=10**6, name="mix"
    )(selection, style, jnp.transpose(bank, (0, 2, 1, 3)))
    final_z = swap_z(final)
    final_c = swap_core(final)
    final_cz = swap_core(final_z)

    grad, ends = call(
        grad_body,
        (shape((taps, NC, groups, 16, channels), F32), shape((2, width, channels), BF16)),
        [SMEM, VMEM, VMEM],
        [
            pltpu.VMEM((NC, groups, 16, (rows + 2) * width), BF16),
            pltpu.VMEM((3, rows * width, channels), BF16),
        ],
        flops=2 * 9 * rows * width * channels * channels,
        nbytes=4 * rows * width * channels,
        vmem=24 << 20,
        name="grad",
    )(place, cot, fm)
    mine, theirs = call(
        edge_body,
        (shape((groups,) + piece, F32), shape((groups,) + piece, BF16)),
        [SMEM] + [VMEM] * 5,
        [pltpu.VMEM((NC, groups, 16, width), BF16)] * 2,
        flops=2 * 6 * width * channels * channels,
        nbytes=4 * 10**6,
        name="edge",
    )(place, grad, ends, low, high, final_z)

    own_x, one, two, three = call(
        split_x_body,
        (shape(pair, F32),) + (shape(pair, BF16),) * 3,
        [SMEM] + [VMEM] * 2,
        flops=10**6,
        nbytes=3 * 10**6,
        name="split_x",
    )(place, mine, swap_core(theirs))
    x_got = two_first(shift_x, one, two, three)
    total, other = call(
        split_z_body,
        (shape(piece, F32), shape(message_of, BF16)),
        [SMEM] + [VMEM] * 9,
        flops=10**6,
        nbytes=10**6,
        name="split_z",
    )(place, style, own_x, *x_got, final, final_z, final_c, final_cz)
    message, style_row = call(
        owner_body,
        (shape(message_of, BF16), shape((8, channels), F32)),
        [SMEM] + [VMEM] * 5,
        flops=10**6,
        nbytes=10**6,
        name="owner",
    )(selection, style, kernel, total, other, swap_z(other))

    kernels = call(
        kernels_body,
        shape((NZ * NC * taps + 1, own_out, channels), BF16),
        [VMEM] * 5,
        flops=10**9,
        nbytes=10**7,
        name="kernels",
    )(style_row, final, final_c, final_z, final_cz)
    finals = [kernels] + two_first(shift_x, kernels, kernels, kernels)

    over_l = [flip_l(message, k) for k in (1, 3, 2)]
    ahead = call(ahead_body, shape((NL,) + message_of, BF16), [VMEM] * NL, name="ahead")(message, *over_l)
    over_y = two_first(shift_y, ahead, ahead, ahead)

    input_grad, token = call(
        input_body,
        (shape((rows, width, channels), BF16), shape((8, 128), F32)),
        [SMEM] + [VMEM] * (NX + 4),
        [
            pltpu.VMEM((3, channels, 3 * channels), BF16),
            pltpu.VMEM((rows, width, channels), BF16),
            dma((8,)),
        ],
        flops=2 * 9 * rows * width * channels * channels,
        nbytes=4 * rows * width * channels,
        vmem=24 << 20,
        out=(HBM, VMEM),
        name="input",
    )(place, *finals, low, high, cot, ahead)

    style_part = call(style_body, shape((8, channels), F32), [VMEM] * (NX + 1), name="style")(*finals, token)
    bank_grad, token = pl.pallas_call(
        banks_body,
        out_shape=(shape((banks,) + piece, F32), shape((8, 128), F32)),
        in_specs=[VMEM] * NY,
        out_specs=(HBM, VMEM),
        scratch_shapes=[pltpu.VMEM((banks,) + piece, F32), dma((taps,))],
        compiler_params=pltpu.CompilerParams(vmem_limit_bytes=16 << 20),
        cost_estimate=pl.CostEstimate(flops=10**7, bytes_accessed=3 * 10**6, transcendentals=0),
        name="banks",
    )(ahead, *over_y)
    style_grad = call(add_body, shape((1, channels), F32), [VMEM] * 3, name="add")(
        style_part, swap_core(style_part), token
    )

    return (
        input_grad.reshape(feature_map.shape),
        style_grad,
        jnp.transpose(bank_grad, (0, 2, 1, 3)),
    )


def solution(mesh):
    in_specs = (
        P("img", "tile", None, None),
        P("img", "tile", None, None),
        P("img", None),
        P(None, "tile", None, None),
        P("img", None),
    )
    out_specs = (P("img", "tile", None, None), P("img", None), P(None, "tile", None, None))
    return jax.shard_map(local, mesh=mesh, in_specs=in_specs, out_specs=out_specs, check_vma=False)
```
